32 devices in a mesh: dp: 8 (over y, x, core), expert: 4 (over z).
Axes of the slice: x: 2, y: 2, z: 4, core: 2. Of those that a mesh axis runs over, the one named last changes fastest.
Arguments:
- tokens: bfloat16 [4096, 1440], P(('dp', 'expert')), may hold values from -6 to 6
- expert_ids: int32 [4096, 2], P(('dp', 'expert')), may hold values from 0 to 3, all different within a row; in each aligned block of 128 rows (0 to 127, 128 to 255, ...) at most 128 rows name the same one
- combine_weights: float32 [4096, 2], P(('dp', 'expert')), may hold values from 0.2 to 1
- out_grad: bfloat16 [4096, 1440], P(('dp', 'expert')), may hold values from -6 to 6
- w_gate_up: bfloat16 [4, 1440, 2880], P('expert', 'dp'), may hold values from -0.15625 to 0.15625
- w_down: bfloat16 [4, 1440, 1440], P('expert', 'dp'), may hold values from -0.15625 to 0.15625
Outputs:
- mixed_out: bfloat16 [4096, 1440], P(('dp', 'expert'))
- token_grad: bfloat16 [4096, 1440], P(('dp', 'expert'))
- grad_gate_up: float32 [4, 1440, 2880], P('expert', 'dp')
- grad_down: float32 [4, 1440, 1440], P('expert', 'dp')
The draws below stay inside these ranges and needn't reach their ends.
Inputs may be any that keep to these rules, and one draw needn't show every extreme that they name: `expert_ids`: each token names 2 different experts. The 128 tokens of one device name one expert at most 128 times, and in every draw some device names some expert exactly 128 times.
All inputs are finite; a program needn't handle non-finite values.
Results may differ from the reference program's by a relative error of at most 0.018.
Values may be sent and summed in bfloat16 or wider, within the bound.
No kernel may reach another device: no remote copies, remote signals or barrier semaphores. Data moves between devices by JAX's collectives and lax.ppermute only.
A program may use at most 192 MiB of HBM per device.

```python
import math
import jax
import jax.numpy as jnp
import numpy as np
from jax import lax

D = 1440
FF = 1440
TOP = 2
TOK_DEV = 128
EXPERTS = 4
CAP = 128
TOKENS = 4096
N_DP = 8
N_EXPERT = 4


def steps_of(rng, dims, pieces, least, largest):
    gain, own = 1.0, jax.random.fold_in(rng, 6)
    for dim, parts in pieces:
        heights = jnp.exp(jax.random.uniform(jax.random.fold_in(own, dim), (parts,), jnp.float32, least / len(pieces), largest / len(pieces)))
        gain = gain * jnp.repeat(heights, dims[dim] // parts).reshape([-1 if axis == dim else 1 for axis in range(len(dims))])
    return gain


def shared_out(own_key, own, number, rows, count, top, bound, slope):
    ranking = jax.random.permutation(own_key, count)
    packed, usual = load_shares(count, rows * top, bound, slope, True), load_shares(count, rows * top, bound, slope, False)
    places = jnp.arange(count)

    def named(sizes, rotation):
        used = int((sizes > 0).sum())
        fixed = max(1, used // 4)
        moved = fixed + (places - fixed + rotation * (used - fixed)) % max(1, count - fixed)
        return jnp.zeros((count,), jnp.int32).at[ranking[jnp.where(places < fixed, places, moved)]].set(jnp.asarray(sizes, jnp.int32))

    sizes = jnp.where(number % 4 == 0, named(packed, number // 4), named(usual, number - number // 4 - 1))
    mixed = jax.random.permutation(jax.random.fold_in(own, 3), count)
    donor, taker = mixed[0:count // 2 * 2:2], mixed[1:count // 2 * 2:2]
    margin = jnp.minimum(sizes[donor] - 1, bound - sizes[taker]) // 2
    margin = jnp.where((donor == ranking[0]) | (taker == ranking[0]) | (sizes[taker] == 0), 0, jnp.maximum(margin, 0))
    moved = jax.random.randint(jax.random.fold_in(own, 4), (count // 2,), 0, 1 << 20) % (margin + 1)
    sizes = sizes.at[donor].add(-moved).at[taker].add(moved)
    labels = jnp.searchsorted(jnp.cumsum(sizes), jnp.arange(rows * top), side="right").astype(jnp.int32)
    grid = labels.reshape(top, rows).T
    grid = grid[jax.random.permutation(jax.random.fold_in(own, 1), rows)]
    rotation = jax.random.randint(jax.random.fold_in(own, 2), (rows, 1), 0, top)
    return jnp.take_along_axis(grid, (jnp.arange(top)[None, :] + rotation) % top, axis=1)


def load_shares(amount, total, most, slope, full):
    portions = [(1 << 20) // math.isqrt(rank ** slope) + 1 for rank in range(1, amount + 1)]
    largest = most if full else min(most, max(-(-total // amount), total * portions[0] // sum(portions)))
    least = 1 if total - largest >= amount - 1 else 0
    given, surplus = [largest] + [least] * (amount - 1), total - largest - least * (amount - 1)
    while surplus > 0:
        candidates = [i for i in range(1, amount) if given[i] < largest] or [i for i in range(1, amount) if given[i] < most]
        pool, left = sum([portions[i] for i in candidates]), surplus
        for i in candidates:
            extra = min(most - given[i], max(1, left * portions[i] // pool), surplus)
            given[i] = given[i] + extra
            surplus = surplus - extra
    return np.array(given)


def normal_values(stream_key, shape, spread, bound, shards=(), kind=jnp.bfloat16):
    array = spread * jax.random.normal(stream_key, shape, jnp.float32)
    if shards:
        array = array * steps_of(stream_key, shape, shards, -0.22, 0.18)
    return jnp.clip(array, -bound, bound).astype(kind)


def setup_inputs(seed: int = 0) -> dict:
    keys = jax.random.split(jax.random.key(seed), 7)
    tokens = normal_values(keys[0], (TOKENS, D), 1.0, 6.0, ((0, 32),))
    expert_ids_keys = jax.random.split(jax.random.fold_in(keys[1], 1), TOKENS // TOK_DEV)
    expert_ids_turns = jax.random.permutation(jax.random.fold_in(keys[1], 3), TOKENS // TOK_DEV)
    expert_ids = jax.vmap(lambda own, number: shared_out(jax.random.fold_in(keys[1], 2), own, number, TOK_DEV, EXPERTS, TOP, CAP, 2))(expert_ids_keys, expert_ids_turns).reshape((TOKENS, TOP))
    combine_weights = jnp.clip(0.2 + 0.8 * jax.random.uniform(keys[2], (TOKENS, TOP), jnp.float32) ** steps_of(keys[2], (TOKENS, TOP), ((0, 32),), -0.2, 0.2), 0.2, 1.0)
    out_grad = normal_values(keys[3], (TOKENS, D), 1.0, 6.0, ((0, 32),))
    w_gate_up = normal_values(keys[4], (EXPERTS, D, 2 * FF), D ** -0.5, 0.15625, ((0, 4), (1, 8)))
    w_down = normal_values(keys[5], (EXPERTS, FF, D), FF ** -0.5, 0.15625, ((0, 4), (1, 8)))
    return dict(tokens=tokens, expert_ids=expert_ids, combine_weights=combine_weights, out_grad=out_grad, w_gate_up=w_gate_up, w_down=w_down)


GLU_ALPHA = 1.702

def expert_rows(rows_in, grads_in, weight_gu, weight_down):
    hidden_width = weight_down.shape[0]
    pre_val = jnp.dot(rows_in, weight_gu, preferred_element_type=jnp.float32)
    gate_part = pre_val[:, :hidden_width]
    up_part = pre_val[:, hidden_width:]
    sigmoid_val = jax.nn.sigmoid(GLU_ALPHA * gate_part)
    glu_val = gate_part * sigmoid_val
    hidden = ((up_part + 1.0) * glu_val).astype(jnp.bfloat16)
    expert_out = jnp.dot(hidden, weight_down, preferred_element_type=jnp.float32).astype(jnp.bfloat16)
    hidden_grad = jnp.dot(grads_in, weight_down.T, preferred_element_type=jnp.float32)
    up_grad = hidden_grad * glu_val
    gate_grad = hidden_grad * (up_part + 1.0) * (sigmoid_val + GLU_ALPHA * gate_part * sigmoid_val * (1.0 - sigmoid_val))
    pre_grad = jnp.concatenate([gate_grad, up_grad], axis=1).astype(jnp.bfloat16)
    input_grad = jnp.dot(pre_grad, weight_gu.T, preferred_element_type=jnp.float32).astype(jnp.bfloat16)
    return (expert_out, input_grad, hidden, pre_grad)

def reference(tokens, expert_ids, combine_weights, out_grad, w_gate_up, w_down):
    group_rows = TOK_DEV * N_EXPERT
    slot_rows = N_EXPERT * CAP
    flat_rows = group_rows * TOP
    grad_scale = 1.0 / math.sqrt(N_DP * TOK_DEV * TOP)
    tokens_grouped = tokens.reshape(N_DP, group_rows, D)
    ids_grouped = expert_ids.reshape(N_DP, flat_rows)
    weights_grouped = combine_weights.reshape(N_DP, flat_rows)
    grads_grouped = out_grad.reshape(N_DP, group_rows, D)
    owner_of = jnp.arange(flat_rows, dtype=jnp.int32) // TOP

    def per_group(totals, inputs):
        group_tokens, group_ids, group_weights, group_grads = inputs
        row_grads = (group_weights[:, None] * group_grads[owner_of].astype(jnp.float32)).astype(jnp.bfloat16)
        mixed_sum = jnp.zeros((group_rows, D), jnp.float32)
        token_sum = jnp.zeros((group_rows, D), jnp.float32)
        total_gu, total_down = totals
        for expert_no in range(N_EXPERT):
            chosen = group_ids == expert_no
            slot_rank = jnp.cumsum(chosen.astype(jnp.int32)) - 1
            places = jnp.where(chosen, slot_rank, slot_rows).astype(jnp.int32)
            picked = jnp.full((slot_rows,), flat_rows, jnp.int32).at[places].set(jnp.arange(flat_rows, dtype=jnp.int32), mode='drop')
            is_valid = picked < flat_rows
            safe_rows = jnp.minimum(picked, flat_rows - 1)
            safe_tokens = safe_rows // TOP
            rows_in = jnp.where(is_valid[:, None], group_tokens[safe_tokens], 0).astype(group_tokens.dtype)
            grads_in = jnp.where(is_valid[:, None], row_grads[safe_rows], 0).astype(row_grads.dtype)
            expert_out, input_grad, hidden, pre_grad = expert_rows(rows_in, grads_in, w_gate_up[expert_no], w_down[expert_no])
            row_weight = jnp.where(is_valid, group_weights[safe_rows], 0.0)
            mixed_sum = mixed_sum.at[safe_tokens].add(row_weight[:, None] * expert_out.astype(jnp.float32))
            token_sum = token_sum.at[safe_tokens].add(jnp.where(is_valid[:, None], input_grad.astype(jnp.float32), 0.0))
            part_gu = jnp.dot(rows_in.T, pre_grad, preferred_element_type=jnp.float32) * grad_scale
            part_down = jnp.dot(hidden.T, grads_in, preferred_element_type=jnp.float32) * grad_scale
            rounded_gu = lax.optimization_barrier(part_gu.astype(jnp.bfloat16)).astype(jnp.float32)
            rounded_down = lax.optimization_barrier(part_down.astype(jnp.bfloat16)).astype(jnp.float32)
            total_gu = total_gu.at[expert_no].add(rounded_gu)
            total_down = total_down.at[expert_no].add(rounded_down)
        return ((total_gu, total_down), (mixed_sum.astype(jnp.bfloat16), token_sum.astype(jnp.bfloat16)))
    start_totals = (jnp.zeros((N_EXPERT, D, 2 * FF), jnp.float32), jnp.zeros((N_EXPERT, FF, D), jnp.float32))
    totals, outputs = lax.scan(per_group, start_totals, (tokens_grouped, ids_grouped, weights_grouped, grads_grouped))
    mixed_out = outputs[0].reshape(TOKENS, D)
    token_grad = outputs[1].reshape(TOKENS, D)
    return (mixed_out, token_grad, totals[0], totals[1])
```

```python
import math

import jax
import jax.numpy as jnp
from jax import lax
from jax.sharding import PartitionSpec as P

GLU_ALPHA = 1.702
BF = jnp.bfloat16
F32 = jnp.float32


def route_matrix(expert_ids, combine_weights, experts):
    hit = expert_ids[:, :, None] == jnp.arange(experts, dtype=jnp.int32)[None, None, :]
    return jnp.sum(jnp.where(hit, combine_weights[:, :, None], 0.0), axis=1)


def dense_forward(rows, weight_gu):
    half = weight_gu.shape[1] // 2
    pre = jnp.dot(rows, weight_gu, preferred_element_type=F32)
    gate, up = pre[:, :half], pre[:, half:]
    sig = jax.nn.sigmoid(GLU_ALPHA * gate)
    glu = gate * sig
    hidden = ((up + 1.0) * glu).astype(BF)
    gate_factor = (up + 1.0) * (sig + GLU_ALPHA * gate * sig * (1.0 - sig))
    return hidden, glu, gate_factor


def contract(left, right, dims):
    return lax.dot_general(left, right, ((dims[:1], dims[1:]), ((), ())), preferred_element_type=F32)


def general(tokens, expert_ids, combine_weights, out_grad, w_gate_up, w_down):
    experts = lax.axis_size("expert")
    replicas = lax.axis_size("dp")
    count, top = expert_ids.shape
    scale = 1.0 / math.sqrt(replicas * count * top)
    me = lax.axis_index("expert")
    table = route_matrix(expert_ids, combine_weights, experts)
    rows = lax.all_gather(tokens, "expert", axis=0, tiled=True)
    grads = lax.all_gather(out_grad, "expert", axis=0, tiled=True)
    table = lax.all_gather(table, "expert", axis=0, tiled=True)
    weight = lax.dynamic_slice_in_dim(table, me, 1, 1)
    row_grad = (weight * grads.astype(F32)).astype(BF)
    weight_gu = lax.all_gather(w_gate_up[0], "dp", axis=0, tiled=True)
    weight_down = lax.all_gather(w_down[0], "dp", axis=0, tiled=True)
    hidden, glu, gate_factor = dense_forward(rows, weight_gu)
    expert_out = jnp.dot(hidden, weight_down, preferred_element_type=F32).astype(BF)
    mixed = (weight * expert_out.astype(F32)).astype(BF)
    hidden_grad = contract(row_grad, weight_down, (1, 1))
    pre_grad = jnp.concatenate([hidden_grad * gate_factor, hidden_grad * glu], axis=1).astype(BF)
    input_grad = contract(pre_grad, weight_gu, (1, 1)).astype(BF)
    part_gu = (contract(rows, pre_grad, (0, 0)) * scale).astype(BF)
    part_down = (contract(hidden, row_grad, (0, 0)) * scale).astype(BF)

    def scatter(value, axis):
        return lax.psum_scatter(value, axis, scatter_dimension=0, tiled=True)

    return (
        scatter(mixed, "expert"),
        scatter(input_grad, "expert"),
        scatter(part_gu, "dp").astype(F32)[None],
        scatter(part_down, "dp").astype(F32)[None],
    )


def paired(tokens, expert_ids, combine_weights, out_grad, w_gate_up, w_down):
    count, top = expert_ids.shape
    width = tokens.shape[1]
    scale = 1.0 / math.sqrt(8 * count * top)
    place = lax.axis_index("dp")
    line = lax.axis_index("expert")
    core, col, row = place % 2, (place // 2) % 2, place // 4
    block = w_gate_up.shape[1]
    hidden_width = w_gate_up.shape[2] // 2
    mine = hidden_width // 2

    def swap(bit):
        pairs = [(i, i ^ bit) for i in range(8)]
        return lambda value: lax.ppermute(value, "dp", pairs)

    over_core, over_x, over_y = swap(1), swap(2), swap(4)

    def right(value, senders=3):
        return lax.ppermute(value, "expert", [(i, i + 1) for i in range(senders)])

    def left(value, senders=3):
        return lax.ppermute(value, "expert", [(3 - i, 2 - i) for i in range(senders)])

    def line_gather(value):
        r1, l1 = right(value), left(value)
        r2, l2 = right(r1), left(l1)
        r3, l3 = right(r2), left(l2)
        return jnp.concatenate([value, l1 + r3, l2 + r2, l3 + r1], axis=0)

    table = lax.all_gather(route_matrix(expert_ids, combine_weights, 4), "expert", axis=0)
    weight = lax.dynamic_index_in_dim(table, line, 2, keepdims=False)
    weight = jnp.concatenate(
        [lax.dynamic_index_in_dim(weight, (line + s) % 4, 0, keepdims=False) for s in range(4)]
    )[:, None]

    pieces = [w_gate_up[0][:, j * block : (j + 1) * block] for j in range(16)]
    even = jnp.concatenate(pieces[0::2], axis=1)
    odd = jnp.concatenate(pieces[1::2], axis=1)
    own = jnp.where(core == 0, even, odd)
    other = over_core(jnp.where(core == 0, odd, even))

    cut = block // 32 * 16 + 16

    def chip_gather(first, second):
        fx, sy = over_x(first), over_y(second)
        fy, sx = over_y(first), over_x(second)
        fxy, sxy = over_y(fx), over_x(sy)
        return (first, fx, fy, fxy), (second, sx, sy, sxy)

    def chips():
        for k in range(4):
            yield k, row ^ (k // 2), col ^ (k % 2)

    own_all, other_all = chip_gather(own, other)
    top_all, low_all = chip_gather(w_down[0][:cut], w_down[0][cut:])
    weight_gu = jnp.zeros((width, 2 * mine), BF)
    weight_down = jnp.zeros((mine, width), BF)
    for k, at_row, at_col in chips():
        chip = at_row * 2 + at_col
        weight_gu = lax.dynamic_update_slice_in_dim(weight_gu, own_all[k], (chip * 2 + core) * block, 0)
        weight_gu = lax.dynamic_update_slice_in_dim(weight_gu, other_all[k], (chip * 2 + 1 - core) * block, 0)
        weight_down = lax.dynamic_update_slice_in_dim(weight_down, top_all[k], chip * block, 0)
        weight_down = lax.dynamic_update_slice_in_dim(weight_down, low_all[k], chip * block + cut, 0)

    rows_own = line_gather(tokens)
    rows = jnp.concatenate([rows_own, over_core(rows_own)], axis=0)
    grads_own = (weight * line_gather(out_grad).astype(F32)).astype(BF)
    row_grad = jnp.concatenate([grads_own, over_core(grads_own)], axis=0)

    hidden, glu, gate_factor = dense_forward(rows, weight_gu)
    part_down = (contract(hidden, row_grad, (0, 0)) * scale).astype(BF)
    hidden_grad = contract(row_grad, weight_down, (1, 1))
    pre_grad = jnp.concatenate([hidden_grad * gate_factor, hidden_grad * glu], axis=1).astype(BF)
    part_gu = (contract(rows, pre_grad, (0, 0)) * scale).astype(BF)
    out_part = jnp.dot(hidden, weight_down, preferred_element_type=F32)
    in_part = contract(pre_grad, weight_gu, (1, 1))

    half = 4 * count

    def pair_sum(value):
        return value[:half] + over_core(value[half:].astype(BF)).astype(F32)

    def line_scatter(value):
        slot = [value[s * count : (s + 1) * count] for s in range(4)]
        r = right(slot[3], 1)
        l = left(slot[1], 1)
        r = right(slot[2] + r, 2)
        l = left(slot[2] + l, 2)
        r = right(slot[1] + r, 3)
        l = left(slot[3] + l, 3)
        return (slot[0].astype(F32) + r.astype(F32) + l.astype(F32)).astype(BF)

    mixed_out = line_scatter((weight * pair_sum(out_part)).astype(BF))
    token_grad = line_scatter(pair_sum(in_part).astype(BF))

    def chip_scatter(get, first_over, second_over, near, far, both):
        sent = first_over(jnp.stack([get(*near), get(*both)]))
        keep = get(row, col).astype(F32) + sent[0].astype(F32)
        away = (get(*far).astype(F32) + sent[1].astype(F32)).astype(BF)
        return keep + second_over(away).astype(F32)

    spot = (row, 1 - col), (1 - row, col), (1 - row, 1 - col)

    def get_gu(which):
        return lambda r, c: lax.dynamic_slice_in_dim(part_gu, ((r * 2 + c) * 2 + which) * block, block, 0)

    def get_down(start, size):
        return lambda r, c: lax.dynamic_slice_in_dim(part_down, (r * 2 + c) * block + start, size, 0)

    down_a = chip_scatter(get_down(0, cut), over_x, over_y, *spot)
    down_b = chip_scatter(get_down(cut, block - cut), over_y, over_x, spot[1], spot[0], spot[2])
    gu_a = chip_scatter(get_gu(0), over_x, over_y, *spot)
    gu_b = chip_scatter(get_gu(1), over_y, over_x, spot[1], spot[0], spot[2])
    keep = jnp.where(core == 0, gu_a, gu_b)
    got = over_core(jnp.where(core == 0, gu_b, gu_a).astype(BF)).astype(F32)
    even = jnp.where(core == 0, keep, got)
    odd = jnp.where(core == 0, got, keep)
    grad_gate_up = jnp.concatenate(
        [part[:, j * block : (j + 1) * block] for j in range(8) for part in (even, odd)], axis=1
    )
    return (mixed_out, token_grad, grad_gate_up[None], jnp.concatenate([down_a, down_b], axis=0)[None])


def solution(mesh):
    placed = (
        P(("dp", "expert"), None),
        P(("dp", "expert"), None),
        P(("dp", "expert"), None),
        P(("dp", "expert"), None),
        P("expert", "dp", None),
        P("expert", "dp", None),
    )
    small = mesh.shape["dp"] == 8 and mesh.shape["expert"] == 4
    return jax.shard_map(
        paired if small else general,
        mesh=mesh,
        in_specs=placed,
        out_specs=(
            P(("dp", "expert"), None),
            P(("dp", "expert"), None),
            P("expert", "dp", None),
            P("expert", "dp", None),
        ),
        check_vma=False,
    )
```

```python
import functools
import math

import jax
import jax.numpy as jnp
from jax import lax
from jax.experimental import pallas as pl
from jax.experimental.pallas import tpu as pltpu
from jax.sharding import PartitionSpec as P

GLU_ALPHA = 1.702
BF = jnp.bfloat16
F32 = jnp.float32


def route_matrix(expert_ids, combine_weights, experts):
    hit = expert_ids[:, :, None] == jnp.arange(experts, dtype=jnp.int32)[None, None, :]
    return jnp.sum(jnp.where(hit, combine_weights[:, :, None], 0.0), axis=1)


def dense_forward(rows, weight_gu):
    half = weight_gu.shape[1] // 2
    pre = jnp.dot(rows, weight_gu, preferred_element_type=F32)
    gate, up = pre[:, :half], pre[:, half:]
    sig = jax.nn.sigmoid(GLU_ALPHA * gate)
    glu = gate * sig
    hidden = ((up + 1.0) * glu).astype(BF)
    gate_factor = (up + 1.0) * (sig + GLU_ALPHA * gate * sig * (1.0 - sig))
    return hidden, glu, gate_factor


def contract(left, right, dims):
    return lax.dot_general(left, right, ((dims[:1], dims[1:]), ((), ())), preferred_element_type=F32)


def general(tokens, expert_ids, combine_weights, out_grad, w_gate_up, w_down):
    experts = lax.axis_size("expert")
    replicas = lax.axis_size("dp")
    count, top = expert_ids.shape
    scale = 1.0 / math.sqrt(replicas * count * top)
    me = lax.axis_index("expert")
    table = route_matrix(expert_ids, combine_weights, experts)
    rows = lax.all_gather(tokens, "expert", axis=0, tiled=True)
    grads = lax.all_gather(out_grad, "expert", axis=0, tiled=True)
    table = lax.all_gather(table, "expert", axis=0, tiled=True)
    weight = lax.dynamic_slice_in_dim(table, me, 1, 1)
    row_grad = (weight * grads.astype(F32)).astype(BF)
    weight_gu = lax.all_gather(w_gate_up[0], "dp", axis=0, tiled=True)
    weight_down = lax.all_gather(w_down[0], "dp", axis=0, tiled=True)
    hidden, glu, gate_factor = dense_forward(rows, weight_gu)
    expert_out = jnp.dot(hidden, weight_down, preferred_element_type=F32).astype(BF)
    mixed = (weight * expert_out.astype(F32)).astype(BF)
    hidden_grad = contract(row_grad, weight_down, (1, 1))
    pre_grad = jnp.concatenate([hidden_grad * gate_factor, hidden_grad * glu], axis=1).astype(BF)
    input_grad = contract(pre_grad, weight_gu, (1, 1)).astype(BF)
    part_gu = (contract(rows, pre_grad, (0, 0)) * scale).astype(BF)
    part_down = (contract(hidden, row_grad, (0, 0)) * scale).astype(BF)

    def scatter(value, axis):
        return lax.psum_scatter(value, axis, scatter_dimension=0, tiled=True)

    return (
        scatter(mixed, "expert"),
        scatter(input_grad, "expert"),
        scatter(part_gu, "dp").astype(F32)[None],
        scatter(part_down, "dp").astype(F32)[None],
    )


PAD = 192
TOP_ROWS = 96
VMEM_LIMIT = 58 * 1024 * 1024


def zeros(shape, dtype=F32):
    return jnp.zeros(shape, dtype)


def prepare_kernel(spot, tokens_t, grads_t, ids_t, weights_t, w_gu, w_down, first, other, low, packed):
    core = spot[0]
    width, count = tokens_t.shape
    block = w_gu.shape[0]
    blocks = width // block
    gap = PAD - block
    full = blocks * PAD

    x = tokens_t[...].astype(F32)
    spread = []
    for i in range(blocks):
        spread += [x[i * block : (i + 1) * block], zeros((gap, count))]
    packed[:, :full] = jnp.concatenate(spread, axis=0).T.astype(BF)

    hit = [ids_t[...] == e for e in range(4)]
    table = jnp.concatenate(
        [jnp.sum(jnp.where(h, weights_t[...], 0.0), axis=0, keepdims=True) for h in hit], axis=0
    )
    high = table.astype(BF).astype(F32)
    rows = [grads_t[...].astype(F32), high, table - high, zeros((full - width - 8, count))]
    packed[:, full:] = jnp.concatenate(rows, axis=0).T.astype(BF)

    w = w_gu[...]
    edge = zeros((block, gap), BF)

    def half(parity):
        parts = []
        for j in range(blocks):
            at = (2 * j + parity) * block
            parts += [w[:, at : at + block], edge]
        return jnp.concatenate(parts, axis=1)

    even, odd = half(0), half(1)
    bottom = zeros((gap, full), BF)
    first[:block, :] = jnp.where(core == 0, even, odd)
    first[block:PAD, :] = bottom
    other[:block, :] = jnp.where(core == 0, odd, even)
    other[block:, :] = bottom
    side = zeros((block, full - width), BF)
    down = jnp.concatenate([w_down[...], side], axis=1)
    first[PAD:, :] = down[:TOP_ROWS]
    low[: block - TOP_ROWS, :] = down[TOP_ROWS:]
    low[block - TOP_ROWS :, :] = bottom


def start_all(copies):
    for c in copies:
        c.start()
    return copies


def wait_all(copies):
    for c in copies:
        c.wait()


def weight_copies(spot, firsts, seconds, w_gu, w_down, sems):
    core, chip = spot[0], spot[1]
    gu, down = [], []
    for k in range(4):
        j = jnp.bitwise_xor(chip, k)
        pairs = (
            (gu, firsts[k].at[pl.ds(0, PAD)], w_gu.at[pl.ds(pl.multiple_of((2 * j + core) * PAD, PAD), PAD)]),
            (gu, seconds[k].at[pl.ds(0, PAD)], w_gu.at[pl.ds(pl.multiple_of((2 * j + 1 - core) * PAD, PAD), PAD)]),
            (down, firsts[k].at[pl.ds(PAD, 96)], w_down.at[pl.ds(pl.multiple_of(j * PAD, PAD), 96)]),
            (down, seconds[k].at[pl.ds(PAD, 96)], w_down.at[pl.ds(pl.multiple_of(j * PAD + 96, 96), 96)]),
        )
        for n, (group, a, b) in enumerate(pairs):
            group.append(pltpu.make_async_copy(a, b, sems.at[4 * k + n]))
    return gu, down


def row_copies(pieces, start, scratch, sems):
    count = pieces[0].shape[0]
    wide = scratch.shape[1]
    return [
        pltpu.make_async_copy(
            p.at[:, pl.ds(start, wide)], scratch.at[pl.ds(n * count, count)], sems.at[n]
        )
        for n, p in enumerate(pieces)
    ]


def forward_kernel(scale, *refs):
    spot = refs[0]
    firsts, seconds, pieces = refs[1:5], refs[5:9], refs[9:17]
    grad_out, up_out, gate_out, out_own, out_far, send_a, keep_a, send_b, keep_b = refs[17:26]
    w_gu, w_down, x, g, hid, up_f, gate_f, out, part, in_sems, x_sems, g_sems, out_sems = refs[26:]
    line, chip = spot[2], spot[1]
    gu, down = weight_copies(spot, firsts, seconds, w_gu, w_down, in_sems)
    full = x.shape[1]
    total = x.shape[0]
    xs = row_copies(pieces, 0, x, x_sems)
    gs = row_copies(pieces, full, g, g_sems)
    start_all(gu)
    start_all(xs)
    start_all(gs)
    start_all(down)
    wait_all(gu)
    wait_all(xs)
    half = w_gu.shape[1] // 2
    step = 256
    lane = lax.broadcasted_iota(jnp.int32, (step, 128), 1)
    picked = (lane == 32 + line) | (lane == 36 + line)
    tail = full - 128
    for m in range(0, total, step):
        at = pl.ds(m, step)
        pre = jnp.dot(x[at, :], w_gu[...], preferred_element_type=F32)
        gate, up = pre[:, :half], pre[:, half:] + 1.0
        sig = jax.nn.sigmoid(GLU_ALPHA * gate)
        glu = gate * sig
        hid[at, :] = (up * glu).astype(BF)
        up_f[at, :] = glu.astype(BF)
        gate_f[at, :] = (up * (sig + GLU_ALPHA * glu * (1.0 - sig))).astype(BF)
    outs = [
        pltpu.make_async_copy(up_f, up_out, out_sems.at[0]),
        pltpu.make_async_copy(gate_f, gate_out, out_sems.at[1]),
    ]
    start_all(outs)
    wait_all(gs)
    wait_all(down)
    for m in range(0, total, step):
        at = pl.ds(m, step)
        out[at, :] = jnp.dot(hid[at, :], w_down[...], preferred_element_type=F32).astype(BF)
        edge = g[at, pl.ds(tail - 0, 128)].astype(F32)
        weight = jnp.sum(jnp.where(picked, edge, 0.0), axis=1, keepdims=True)
        g[at, :] = (weight * g[at, :].astype(F32)).astype(BF)
    own = total // 2
    more = [
        pltpu.make_async_copy(g, grad_out, out_sems.at[2]),
        pltpu.make_async_copy(out.at[pl.ds(0, own)], out_own, out_sems.at[3]),
        pltpu.make_async_copy(out.at[pl.ds(own, own)], out_far, out_sems.at[4]),
    ]
    start_all(more)
    outs += more
    for m in range(0, part.shape[0], 256):
        at = pl.ds(m, 256)
        acc = contract(hid[:, at], g[...], (0, 0))
        part[at, :] = (acc * scale).astype(BF)
    outs += start_all(scatter_copies(chip, part, 1, (0,), (96,), send_a, keep_a, send_b, keep_b, out_sems, 5))
    wait_all(outs)


def scatter_copies(chip, part, stride, a_at, b_at, send_a, keep_a, send_b, keep_b, sems, base):
    size = send_a.shape[1]
    (a_at,), (b_at,) = a_at, b_at
    copies = []
    plan_a = ((0, keep_a, 0), (2, keep_a, 1), (1, send_a, 0), (3, send_a, 1))
    plan_b = ((0, keep_b, 0), (1, keep_b, 1), (2, send_b, 0), (3, send_b, 1))
    for at, plan in ((a_at, plan_a), (b_at, plan_b)):
        for rel, ref, slot in plan:
            row = jnp.bitwise_xor(chip, rel) * (stride * PAD) + at
            source = part.at[pl.ds(pl.multiple_of(row, 96), size)]
            copies.append(pltpu.make_async_copy(source, ref.at[slot], sems.at[base + len(copies)]))
    return copies


def backward_kernel(scale, *refs):
    spot = refs[0]
    firsts, seconds, pieces = refs[1:5], refs[5:9], refs[9:17]
    grad_in, up_in, gate_in = refs[17:20]
    in_own, in_far, send_a, keep_a, send_b, keep_b = refs[20:26]
    w_gu, w_down, x, g, up_f, gate_f, pre_grad, out, part, in_sems, x_sems, out_sems = refs[26:]
    chip = spot[1]
    gu, down = weight_copies(spot, firsts, seconds, w_gu, w_down, in_sems)
    xs = row_copies(pieces, 0, x, x_sems)
    held = [
        pltpu.make_async_copy(grad_in, g, out_sems.at[0]),
        pltpu.make_async_copy(up_in, up_f, out_sems.at[1]),
        pltpu.make_async_copy(gate_in, gate_f, out_sems.at[2]),
    ]
    start_all(down)
    start_all(held)
    start_all(xs)
    start_all(gu)
    wait_all(down)
    wait_all(held)
    total = x.shape[0]
    half = w_gu.shape[1] // 2
    step = 256
    for m in range(0, total, step):
        at = pl.ds(m, step)
        hidden_grad = contract(g[at, :], w_down[...], (1, 1))
        pre_grad[at, :half] = (hidden_grad * gate_f[at, :].astype(F32)).astype(BF)
        pre_grad[at, half:] = (hidden_grad * up_f[at, :].astype(F32)).astype(BF)
    wait_all(xs)
    for m in range(0, part.shape[0], 2 * PAD):
        at = pl.ds(m, 2 * PAD)
        acc = contract(x[:, at], pre_grad[...], (0, 0))
        part[at, :] = (acc * scale).astype(BF)
    outs = start_all(scatter_copies(chip, part, 2, (0,), (PAD,), send_a, keep_a, send_b, keep_b, out_sems, 5))
    wait_all(gu)
    for m in range(0, total, step):
        at = pl.ds(m, step)
        out[at, :] = contract(pre_grad[at, :], w_gu[...], (1, 1)).astype(BF)
    own = total // 2
    outs += start_all([
        pltpu.make_async_copy(out.at[pl.ds(0, own)], in_own, out_sems.at[3]),
        pltpu.make_async_copy(out.at[pl.ds(own, own)], in_far, out_sems.at[4]),
    ])
    wait_all(outs)


def finish_rows_kernel(spread, keep, got, out_t):
    width = out_t.shape[0]
    total = (keep[...].astype(F32) + got[...].astype(F32)).T
    if spread:
        block = width // 8
        total = jnp.concatenate([total[i * PAD : i * PAD + block] for i in range(8)], axis=0)
    out_t[...] = total[:width].astype(BF)


def finish_gate_up_kernel(spot, keep, got, out):
    core = spot[0]
    block = out.shape[0]
    mine = keep[...].astype(F32)[:block]
    theirs = got[...].astype(F32)[:block]
    even = jnp.where(core == 0, mine, theirs)
    odd = jnp.where(core == 0, theirs, mine)
    parts = [p[:, j * PAD : j * PAD + block] for j in range(8) for p in (even, odd)]
    out[...] = jnp.concatenate(parts, axis=1)


VMEM = pl.BlockSpec(memory_space=pltpu.VMEM)
SMEM = pl.BlockSpec(memory_space=pltpu.SMEM)
ANY = pl.BlockSpec(memory_space=pl.ANY)


def call(body, in_specs, out_specs, out_shape, scratch=(), flops=0, touched=0):
    return pl.pallas_call(
        body,
        in_specs=in_specs,
        out_specs=out_specs,
        out_shape=out_shape,
        scratch_shapes=list(scratch),
        compiler_params=pltpu.CompilerParams(vmem_limit_bytes=VMEM_LIMIT),
        cost_estimate=pl.CostEstimate(flops=flops, bytes_accessed=touched, transcendentals=0),
    )


def paired(tokens, expert_ids, combine_weights, out_grad, w_gate_up, w_down):
    count, top = expert_ids.shape
    width = tokens.shape[1]
    scale = 1.0 / math.sqrt(8 * count * top)
    place = lax.axis_index("dp")
    line = lax.axis_index("expert")
    core = place % 2
    spot = jnp.stack([core, place // 2, line]).astype(jnp.int32)
    block = w_gate_up.shape[1]
    full = 8 * PAD
    rows = 8 * count
    dma = pltpu.SemaphoreType.DMA

    def swap(bit):
        pairs = [(i, i ^ bit) for i in range(8)]
        return lambda value: lax.ppermute(value, "dp", pairs)

    over_core, over_x, over_y = swap(1), swap(2), swap(4)

    def onward(value):
        return lax.ppermute(value, "expert", [(i, (i + 1) % 4) for i in range(4)])

    def backward(value):
        return lax.ppermute(value, "expert", [(i, (i + 3) % 4) for i in range(4)])

    def array(*shape):
        return jax.ShapeDtypeStruct(shape, BF)

    first, other, low, packed = call(
        prepare_kernel,
        [SMEM] + [VMEM] * 6,
        [VMEM] * 4,
        [array(PAD + 96, full), array(PAD, full), array(96, full), array(count, 2 * full)],
        touched=6 << 20,
    )(spot, tokens.T, out_grad.T, expert_ids.T, combine_weights.T, w_gate_up[0], w_down[0])

    together = lax.optimization_barrier
    p1, first_x, first_y, other = onward(packed), over_x(first), over_y(first), over_core(other)
    far0 = over_core(packed)
    second = jnp.concatenate([other, low], axis=0)
    p1, first_x, first_y, second, far0 = together((p1, first_x, first_y, second, far0))
    p2, second_x, second_y, far1 = onward(p1), over_x(second), over_y(second), over_core(p1)
    p2, second_x, second_y, first_x, far1 = together((p2, second_x, second_y, first_x, far1))
    p3, first_xy, second_xy, far2 = onward(p2), over_y(first_x), over_x(second_y), over_core(p2)
    far3 = over_core(p3)

    firsts = (first, first_x, first_y, first_xy)
    seconds = (second, second_x, second_y, second_xy)
    pieces = (packed, p1, p2, p3, far0, far1, far2, far3)

    row_shape, unit_shape = (rows, full), (rows, 4 * PAD)
    grad, up_f, gate_f, out_own, out_far, *down_parts = call(
        functools.partial(forward_kernel, scale),
        [SMEM] + [ANY] * 16,
        [ANY] * 9,
        [array(*row_shape), array(*unit_shape), array(*unit_shape), array(rows // 2, full), array(rows // 2, full)]
        + [array(2, 96, full)] * 4,
        [
            pltpu.VMEM((full, full), BF),
            pltpu.VMEM((4 * PAD, full), BF),
            pltpu.VMEM(row_shape, BF),
            pltpu.VMEM(row_shape, BF),
            pltpu.VMEM(unit_shape, BF),
            pltpu.VMEM(unit_shape, BF),
            pltpu.VMEM(unit_shape, BF),
            pltpu.VMEM(row_shape, BF),
            pltpu.VMEM((4 * PAD, full), BF),
            dma((16,)),
            dma((8,)),
            dma((8,)),
            dma((13,)),
        ],
        flops=9_000_000_000,
        touched=25 << 20,
    )(spot, *firsts, *seconds, *pieces)
    in_own, in_far, *gu_parts = call(
        functools.partial(backward_kernel, scale),
        [SMEM] + [ANY] * 19,
        [ANY] * 6,
        [array(rows // 2, full), array(rows // 2, full)] + [array(2, PAD, full)] * 4,
        [
            pltpu.VMEM((full, full), BF),
            pltpu.VMEM((4 * PAD, full), BF),
            pltpu.VMEM(row_shape, BF),
            pltpu.VMEM(row_shape, BF),
            pltpu.VMEM(unit_shape, BF),
            pltpu.VMEM(unit_shape, BF),
            pltpu.VMEM(row_shape, BF),
            pltpu.VMEM(row_shape, BF),
            pltpu.VMEM((full, full), BF),
            dma((16,)),
            dma((8,)),
            dma((13,)),
        ],
        flops=11_000_000_000,
        touched=30 << 20,
    )(spot, *firsts, *seconds, *pieces, grad, up_f, gate_f)

    def edge_weight(piece):
        tail = lax.dynamic_slice_in_dim(piece, full + width + line, 5, 1).astype(F32)
        return tail[:, :1] + tail[:, 4:]

    weights = [edge_weight(p) for p in pieces[:4]]

    def line_scatter(own, far, scaled):
        far = over_core(far)

        def slot(s):
            at = slice(s * count, (s + 1) * count)
            value = own[at].astype(F32) + far[at].astype(F32)
            return value * weights[s] if scaled else value

        moving = backward(slot(3).astype(BF))
        moving = backward((slot(2) + moving.astype(F32)).astype(BF))
        moving = backward((slot(1) + moving.astype(F32)).astype(BF))
        return call(
            functools.partial(finish_rows_kernel, not scaled),
            [VMEM] * 2,
            VMEM,
            array(width, count),
            touched=1 << 20,
        )(slot(0), moving).T

    def chip_scatter(send, keep, first_over, second_over):
        got = first_over(send).astype(F32)
        away = second_over((keep[1].astype(F32) + got[1]).astype(BF))
        return keep[0].astype(F32) + got[0] + away.astype(F32)

    down_a = chip_scatter(down_parts[0], down_parts[1], over_x, over_y)
    down_b = chip_scatter(down_parts[2], down_parts[3], over_y, over_x)
    mixed_out = line_scatter(out_own, out_far, True)
    gu_a = chip_scatter(gu_parts[0], gu_parts[1], over_x, over_y)
    gu_b = chip_scatter(gu_parts[2], gu_parts[3], over_y, over_x)
    token_grad = line_scatter(in_own, in_far, False)
    keep = jnp.where(core == 0, gu_a, gu_b)
    got = over_core(jnp.where(core == 0, gu_b, gu_a).astype(BF))
    grad_gate_up = call(
        finish_gate_up_kernel,
        [SMEM, VMEM, VMEM],
        VMEM,
        jax.ShapeDtypeStruct((block, 2 * width), F32),
        touched=4 << 20,
    )(spot, keep, got)
    grad_down = jnp.concatenate([down_a, down_b], axis=0)[:block, :width]
    return (mixed_out, token_grad, grad_gate_up[None], grad_down[None])


def solution(mesh):
    placed = (
        P(("dp", "expert"), None),
        P(("dp", "expert"), None),
        P(("dp", "expert"), None),
        P(("dp", "expert"), None),
        P("expert", "dp", None),
        P("expert", "dp", None),
    )
    small = mesh.shape["dp"] == 8 and mesh.shape["expert"] == 4
    return jax.shard_map(
        paired if small else general,
        mesh=mesh,
        in_specs=placed,
        out_specs=(
            P(("dp", "expert"), None),
            P(("dp", "expert"), None),
            P("expert", "dp", None),
            P("expert", "dp", None),
        ),
        check_vma=False,
    )
```

```python
import functools
import math

import jax
import jax.numpy as jnp
from jax import lax
from jax.experimental import pallas as pl
from jax.experimental.pallas import tpu as pltpu
from jax.sharding import PartitionSpec as P

GLU_ALPHA = 1.702
BF = jnp.bfloat16
F32 = jnp.float32


def route_matrix(expert_ids, combine_weights, experts):
    hit = expert_ids[:, :, None] == jnp.arange(experts, dtype=jnp.int32)[None, None, :]
    return jnp.sum(jnp.where(hit, combine_weights[:, :, None], 0.0), axis=1)


def dense_forward(rows, weight_gu):
    half = weight_gu.shape[1] // 2
    pre = jnp.dot(rows, weight_gu, preferred_element_type=F32)
    gate, up = pre[:, :half], pre[:, half:]
    sig = jax.nn.sigmoid(GLU_ALPHA * gate)
    glu = gate * sig
    hidden = ((up + 1.0) * glu).astype(BF)
    gate_factor = (up + 1.0) * (sig + GLU_ALPHA * gate * sig * (1.0 - sig))
    return hidden, glu, gate_factor


def contract(left, right, dims):
    return lax.dot_general(left, right, ((dims[:1], dims[1:]), ((), ())), preferred_element_type=F32)


def general(tokens, expert_ids, combine_weights, out_grad, w_gate_up, w_down):
    experts = lax.axis_size("expert")
    replicas = lax.axis_size("dp")
    count, top = expert_ids.shape
    scale = 1.0 / math.sqrt(replicas * count * top)
    me = lax.axis_index("expert")
    table = route_matrix(expert_ids, combine_weights, experts)
    rows = lax.all_gather(tokens, "expert", axis=0, tiled=True)
    grads = lax.all_gather(out_grad, "expert", axis=0, tiled=True)
    table = lax.all_gather(table, "expert", axis=0, tiled=True)
    weight = lax.dynamic_slice_in_dim(table, me, 1, 1)
    row_grad = (weight * grads.astype(F32)).astype(BF)
    weight_gu = lax.all_gather(w_gate_up[0], "dp", axis=0, tiled=True)
    weight_down = lax.all_gather(w_down[0], "dp", axis=0, tiled=True)
    hidden, glu, gate_factor = dense_forward(rows, weight_gu)
    expert_out = jnp.dot(hidden, weight_down, preferred_element_type=F32).astype(BF)
    mixed = (weight * expert_out.astype(F32)).astype(BF)
    hidden_grad = contract(row_grad, weight_down, (1, 1))
    pre_grad = jnp.concatenate([hidden_grad * gate_factor, hidden_grad * glu], axis=1).astype(BF)
    input_grad = contract(pre_grad, weight_gu, (1, 1)).astype(BF)
    part_gu = (contract(rows, pre_grad, (0, 0)) * scale).astype(BF)
    part_down = (contract(hidden, row_grad, (0, 0)) * scale).astype(BF)

    def scatter(value, axis):
        return lax.psum_scatter(value, axis, scatter_dimension=0, tiled=True)

    return (
        scatter(mixed, "expert"),
        scatter(input_grad, "expert"),
        scatter(part_gu, "dp").astype(F32)[None],
        scatter(part_down, "dp").astype(F32)[None],
    )


PAD = 192
HALF = 96
MAIN = 156
LOT = 80
MIB = 1024 * 1024
LONG = 30_000_000_000


def zeros(shape, dtype=F32):
    return jnp.zeros(shape, dtype)


def prepare_kernel(spot, tokens_t, grads_t, ids_t, weights_t, w_gu, w_down, x_out, g_out, own, other, low, high):
    core = spot[0]
    width, count = tokens_t.shape
    block = w_gu.shape[0]
    blocks = width // block
    gap = PAD - block
    full = blocks * PAD

    x = tokens_t[...].astype(F32)
    spread = []
    for i in range(blocks):
        spread += [x[i * block : (i + 1) * block], zeros((gap, count))]
    x_out[...] = jnp.concatenate(spread, axis=0).T.astype(BF)

    hit = [ids_t[...] == e for e in range(4)]
    table = jnp.concatenate(
        [jnp.sum(jnp.where(h, weights_t[...], 0.0), axis=0, keepdims=True) for h in hit], axis=0
    )
    coarse = table.astype(BF).astype(F32)
    rows = [grads_t[...].astype(F32), coarse, table - coarse, zeros((full - width - 8, count))]
    g_out[...] = jnp.concatenate(rows, axis=0).T.astype(BF)

    w = w_gu[...]
    lot = block - MAIN
    edge = zeros((block, lot // 3), BF)
    slim = zeros((block, lot // 6), BF)

    def half(parity):
        parts = []
        for j in range(blocks):
            at = (2 * j + parity) * block
            parts += [w[:, at : at + MAIN], edge, w[:, at + MAIN : at + MAIN + gap], slim, w[:, at + MAIN + gap : at + block]]
        return jnp.concatenate(parts, axis=1)

    even, odd = half(0), half(1)
    down = jnp.concatenate([w_down[...], zeros((block, full - width), BF)], axis=1)
    own[:block, :] = jnp.where(core == 0, even, odd)
    own[block:, :] = down[MAIN : MAIN + gap]
    other[...] = jnp.concatenate([jnp.where(core == 0, odd, even), zeros((gap, full), BF)], axis=0)
    low[...] = down[:LOT]
    high[...] = jnp.concatenate([down[LOT:MAIN], zeros((2 * LOT - MAIN, full), BF)], axis=0)


def join_kernel(other, w_down, out):
    block = w_down.shape[0]
    gap = PAD - block
    out[...] = other[...]
    side = zeros((gap, out.shape[1] - w_down.shape[1]), BF)
    out[block:, :] = jnp.concatenate([w_down[block - gap :, :], side], axis=1)


def start_all(copies):
    for c in copies:
        c.start()
    return copies


def wait_all(copies):
    for c in copies:
        c.wait()


def gate_up_copies(spot, owns, others, w_gu, sems):
    core, chip = spot[0], spot[1]
    copies = []
    for k in range(4):
        j = jnp.bitwise_xor(chip, k)
        for n, (ref, which) in enumerate(((owns[k], core), (others[k], 1 - core))):
            row = pl.multiple_of((2 * j + which) * PAD, PAD)
            copies.append(pltpu.make_async_copy(ref, w_gu.at[pl.ds(row, PAD)], sems.at[2 * k + n]))
    return copies


def down_copies(spot, owns, others, lows, highs, w_down, sems):
    chip = spot[1]
    copies = []
    for k in range(4):
        base = jnp.bitwise_xor(chip, k) * PAD
        parts = (
            (lows[k], 0, LOT),
            (highs[k], LOT, LOT),
            (owns[k].at[pl.ds(PAD - 16, 16)], 2 * LOT, 16),
            (others[k].at[pl.ds(PAD - 16, 16)], 2 * LOT + 16, 16),
        )
        for ref, at, size in parts:
            row = pl.multiple_of(base + at, 16)
            copies.append(pltpu.make_async_copy(ref, w_down.at[pl.ds(row, size)], sems.at[len(copies)]))
    return copies


def row_copies(pieces, starts, scratch, sems):
    count, wide = pieces[0].shape[0], scratch.shape[1]
    return [
        pltpu.make_async_copy(p.at[:, pl.ds(start, wide)], scratch.at[pl.ds(n * count, count)], sems.at[n])
        for n, (p, start) in enumerate(zip(pieces, starts))
    ]


def chunk_copies(source, target, step, sems, base=0):
    return [
        pltpu.make_async_copy(source.at[pl.ds(m, step)], target.at[pl.ds(m, step)], sems.at[base + m // step])
        for m in range(0, source.shape[0], step)
    ]


STEP = 256
X_AT = (0, 0, 0, 0, 0, 0, 0, 0)
G_AT = (0, 8 * PAD, 8 * PAD, 0, 0, 8 * PAD, 8 * PAD, 0)


def hidden_kernel(*refs):
    spot, owns, others, pieces = refs[0], refs[1:5], refs[5:9], refs[9:17]
    hid_out, up_out, gate_out = refs[17:20]
    w_gu, x, hid, up_f, gate_f, w_sems, x_sems, out_sems = refs[20:]
    gu = start_all(gate_up_copies(spot, owns, others, w_gu, w_sems))
    xs = start_all(row_copies(pieces, X_AT, x, x_sems))
    wait_all(gu)
    half = w_gu.shape[1] // 2
    per = STEP // pieces[0].shape[0]
    outs = [
        chunk_copies(a, b, STEP, out_sems, base)
        for a, b, base in ((hid, hid_out, 0), (up_f, up_out, 4), (gate_f, gate_out, 8))
    ]
    for n in range(x.shape[0] // STEP):
        at = pl.ds(n * STEP, STEP)
        wait_all(xs[n * per : (n + 1) * per])
        pre = jnp.dot(x[at, :], w_gu[...], preferred_element_type=F32)
        gate, up = pre[:, :half], pre[:, half:] + 1.0
        sig = jax.nn.sigmoid(GLU_ALPHA * gate)
        glu = gate * sig
        hid[at, :] = (up * glu).astype(BF)
        up_f[at, :] = glu.astype(BF)
        gate_f[at, :] = (up * (sig + GLU_ALPHA * glu * (1.0 - sig))).astype(BF)
        for group in outs:
            group[n].start()
    for group in outs:
        wait_all(group)


def scatter_copies(chip, part, stride, a_at, b_at, send_a, keep_a, send_b, keep_b, sems):
    size = send_a.shape[1]
    copies = []
    plan_a = ((1, send_a, 0), (3, send_a, 1), (0, keep_a, 0), (2, keep_a, 1))
    plan_b = ((2, send_b, 0), (3, send_b, 1), (0, keep_b, 0), (1, keep_b, 1))
    for at, plan in ((a_at, plan_a), (b_at, plan_b)):
        for rel, ref, slot in plan:
            row = jnp.bitwise_xor(chip, rel) * (stride * PAD) + at
            source = part.at[pl.ds(pl.multiple_of(row, HALF), size)]
            copies.append(pltpu.make_async_copy(source, ref.at[slot], sems.at[len(copies)]))
    return copies


def down_grad_kernel(scale, *refs):
    spot, hid_in, pieces = refs[0], refs[1], refs[2:10]
    grad_out, *parts = refs[10:15]
    hid, g, part, hid_sem, g_sems, grad_sems, part_sems = refs[15:]
    line, chip = spot[2], spot[1]
    gs = start_all(row_copies(pieces, G_AT, g, g_sems))
    load = pltpu.make_async_copy(hid_in, hid, hid_sem.at[0])
    load.start()
    full = g.shape[1]
    lane = lax.broadcasted_iota(jnp.int32, (STEP, 128), 1)
    picked = (lane == 32 + line) | (lane == 36 + line)
    per = STEP // pieces[0].shape[0]
    grads = chunk_copies(g, grad_out, STEP, grad_sems)
    for n in range(g.shape[0] // STEP):
        at = pl.ds(n * STEP, STEP)
        wait_all(gs[n * per : (n + 1) * per])
        edge = g[at, pl.ds(full - 128, 128)].astype(F32)
        weight = jnp.sum(jnp.where(picked, edge, 0.0), axis=1, keepdims=True)
        g[at, :] = (weight * g[at, :].astype(F32)).astype(BF)
        grads[n].start()
    load.wait()
    for m in range(0, part.shape[0], STEP):
        at = pl.ds(m, STEP)
        part[at, :] = (contract(hid[:, at], g[...], (0, 0)) * scale).astype(BF)
    outs = start_all(scatter_copies(chip, part, 1, 0, HALF, *parts, part_sems))
    wait_all(grads)
    wait_all(outs)


def row_outs(out, last, first, rest, own, sems):
    return [
        pltpu.make_async_copy(out.at[pl.ds(7 * last, last)], first, sems.at[0]),
        pltpu.make_async_copy(out.at[pl.ds(4 * last, 3 * last)], rest, sems.at[1]),
        pltpu.make_async_copy(out.at[pl.ds(0, 4 * last)], own, sems.at[2]),
    ]


def gate_grad_kernel(scale, *refs):
    spot, owns, others, lows, highs = refs[0], refs[1:5], refs[5:9], refs[9:13], refs[13:17]
    hid_in, grad_in, up_in, gate_in, pieces = refs[17], refs[18], refs[19], refs[20], refs[21:29]
    out_own, out_first, out_rest, pre_out, *parts = refs[29:37]
    w_down, hid, g, up_f, gate_f, out, pre_grad, x, part = refs[37:46]
    w_sems, in_sems, x_sems, row_sems, out_sems, part_sems = refs[46:]
    down = start_all(down_copies(spot, owns, others, lows, highs, w_down, w_sems))
    loads = [
        start_all(chunk_copies(a, b, STEP, in_sems, base))
        for a, b, base in ((hid_in, hid, 0), (grad_in, g, 4), (up_in, up_f, 8), (gate_in, gate_f, 12))
    ]
    xs = start_all(row_copies(pieces, X_AT, x, x_sems))
    wait_all(down)
    last = out.shape[0] // 8
    wait_all(loads[0])
    for n in (3, 2, 1, 0):
        at = pl.ds(n * STEP, STEP)
        out[at, :] = jnp.dot(hid[at, :], w_down[...], preferred_element_type=F32).astype(BF)
    outs = start_all(row_outs(out, last, out_first, out_rest, out_own, row_sems))
    half = w_down.shape[0]
    pres = chunk_copies(pre_grad, pre_out, STEP, out_sems)
    for n in range(g.shape[0] // STEP):
        at = pl.ds(n * STEP, STEP)
        wait_all([loads[1][n], loads[2][n], loads[3][n]])
        hidden_grad = contract(g[at, :], w_down[...], (1, 1))
        pre_grad[at, :half] = (hidden_grad * gate_f[at, :].astype(F32)).astype(BF)
        pre_grad[at, half:] = (hidden_grad * up_f[at, :].astype(F32)).astype(BF)
        pres[n].start()
    wait_all(xs)
    for m in range(0, part.shape[0], 2 * PAD):
        at = pl.ds(m, 2 * PAD)
        part[at, :] = (contract(x[:, at], pre_grad[:, :half], (0, 0)) * scale).astype(BF)
    outs += start_all(scatter_copies(spot[1], part, 2, 0, PAD, *parts, part_sems))
    wait_all(pres)
    wait_all(outs)


def up_grad_kernel(scale, *refs):
    spot, owns, others, pieces, pre_in = refs[0], refs[1:5], refs[5:9], refs[9:17], refs[17]
    in_own, in_first, in_rest, *parts = refs[18:25]
    w_gu, x, pre_grad, part, out, w_sems, x_sems, in_sems, out_sems, part_sems = refs[25:]
    loads = start_all(chunk_copies(pre_in, pre_grad, STEP, in_sems))
    xs = start_all(row_copies(pieces, X_AT, x, x_sems))
    gu = start_all(gate_up_copies(spot, owns, others, w_gu, w_sems))
    wait_all(loads)
    wait_all(xs)
    half = part.shape[1]
    for m in range(0, part.shape[0], 2 * PAD):
        at = pl.ds(m, 2 * PAD)
        part[at, :] = (contract(x[:, at], pre_grad[:, half:], (0, 0)) * scale).astype(BF)
    outs = start_all(scatter_copies(spot[1], part, 2, 0, PAD, *parts, part_sems))
    wait_all(gu)
    last = out.shape[0] // 8
    for n in (3, 2, 1, 0):
        at = pl.ds(n * STEP, STEP)
        out[at, :] = contract(pre_grad[at, :], w_gu[...], (1, 1)).astype(BF)
    outs += start_all(row_outs(out, last, in_first, in_rest, in_own, out_sems))
    wait_all(outs)


def finish_rows_kernel(spread, keep, got, out_t):
    width = out_t.shape[0]
    total = (keep[...].astype(F32) + got[...].astype(F32)).T
    if spread:
        block = width // 8
        total = jnp.concatenate([total[i * PAD : i * PAD + block] for i in range(8)], axis=0)
    out_t[...] = total[:width].astype(BF)


def finish_gate_up_kernel(spot, gate_keep, gate_far, up_keep, up_far, out):
    core = spot[0]
    block = out.shape[0]
    parts = []
    for keep, far in ((gate_keep, gate_far), (up_keep, up_far)):
        mine = keep[...].astype(F32)[:block]
        theirs = far[...].astype(F32)[:block]
        even = jnp.where(core == 0, mine, theirs)
        odd = jnp.where(core == 0, theirs, mine)
        for j in range(4):
            for p in (even, odd):
                at = j * PAD
                parts += [p[:, at : at + MAIN], p[:, at + 164 : at + 176], p[:, at + 180 : at + PAD]]
    out[...] = jnp.concatenate(parts, axis=1)


VMEM = pl.BlockSpec(memory_space=pltpu.VMEM)
SMEM = pl.BlockSpec(memory_space=pltpu.SMEM)
ANY = pl.BlockSpec(memory_space=pl.ANY)


def call(body, in_specs, out_specs, out_shape, scratch=(), mib=58, flops=1000):
    return pl.pallas_call(
        body,
        in_specs=in_specs,
        out_specs=out_specs,
        out_shape=out_shape,
        scratch_shapes=list(scratch),
        compiler_params=pltpu.CompilerParams(vmem_limit_bytes=mib * MIB),
        cost_estimate=pl.CostEstimate(flops=flops, bytes_accessed=1000, transcendentals=0),
    )


def paired(tokens, expert_ids, combine_weights, out_grad, w_gate_up, w_down):
    count, top = expert_ids.shape
    width = tokens.shape[1]
    scale = 1.0 / math.sqrt(8 * count * top)
    place = lax.axis_index("dp")
    line = lax.axis_index("expert")
    core = place % 2
    spot = jnp.stack([core, place // 2, line]).astype(jnp.int32)
    block = w_gate_up.shape[1]
    full = 8 * PAD
    units = 4 * PAD
    rows = 8 * count
    dma = pltpu.SemaphoreType.DMA

    def swap(bit):
        pairs = [(i, i ^ bit) for i in range(8)]
        return lambda value: lax.ppermute(value, "dp", pairs)

    over_core, over_x, over_y = swap(1), swap(2), swap(4)

    def onward(value):
        return lax.ppermute(value, "expert", [(i, (i + 1) % 4) for i in range(4)])

    def backward(value):
        return lax.ppermute(value, "expert", [(i, (i + 3) % 4) for i in range(4)])

    def array(*shape):
        return jax.ShapeDtypeStruct(shape, BF)

    def held(*shape):
        return pltpu.VMEM(shape, BF)

    def together(*values):
        return lax.optimization_barrier(values)

    x0, g0, own, other, low, high = call(
        prepare_kernel,
        [SMEM] + [VMEM] * 6,
        [VMEM] * 6,
        [array(count, full)] * 2 + [array(PAD, full)] * 2 + [array(LOT, full)] * 2,
    )(spot, tokens.T, out_grad.T, expert_ids.T, combine_weights.T, w_gate_up[0], w_down[0])

    def beside(*values):
        return jnp.concatenate(values, axis=1)

    other, own_x, own_y, x1, fx0 = over_core(other), over_x(own), over_y(own), onward(x0), over_core(x0)
    other = call(join_kernel, [VMEM] * 2, VMEM, array(PAD, full))(other, w_down[0])
    own_x, own_y, x1, other, fx0, g0, low, high = together(own_x, own_y, x1, other, fx0, g0, low, high)
    other_x, other_y, xg2 = over_x(other), over_y(other), onward(beside(x1, g0))
    fx1, fg0 = over_core(x1), over_core(g0)
    other_x, other_y, xg2, fx1, fg0, own_x, low, high = together(other_x, other_y, xg2, fx1, fg0, own_x, low, high)
    own_xy, other_xy, xg3, fxg2 = over_y(own_x), over_x(other_y), onward(xg2), over_core(xg2)
    own_xy, other_xy, xg3, fxg2, low, high = together(own_xy, other_xy, xg3, fxg2, low, high)
    fxg3 = over_core(xg3)
    g3 = onward(xg3[:, full:])
    low_x, high_y, low_y, high_x = over_x(low), over_y(high), over_y(low), over_x(high)

    owns = (own, own_x, own_y, own_xy)
    others = (other, other_x, other_y, other_xy)
    xs = (x0, x1, xg2, xg3, fx0, fx1, fxg2, fxg3)

    hid, up_f, gate_f = call(
        hidden_kernel,
        [SMEM] + [ANY] * 16,
        [ANY] * 3,
        [array(rows, units)] * 3,
        [held(full, full), held(rows, full)] + [held(rows, units)] * 3 + [dma((8,)), dma((8,)), dma((12,))],
        flops=LONG,
    )(spot, *owns, *others, *xs)
    hid, g3, low_x, high_y, low_y, high_x = together(hid, g3, low_x, high_y, low_y, high_x)
    low_xy, high_xy, fg3 = over_y(low_x), over_x(high_y), over_core(g3)
    lows = (low, low_x, low_y, low_xy)
    highs = (high, high_x, high_y, high_xy)
    weights_in = owns + others + lows + highs
    grad, *down_parts = call(
        functools.partial(down_grad_kernel, scale),
        [SMEM] + [ANY] * 9,
        [ANY] * 5,
        [array(rows, full)] + [array(2, HALF, full)] * 4,
        [held(rows, units), held(rows, full), held(units, full), dma((1,)), dma((8,)), dma((4,)), dma((8,))],
        flops=LONG,
    )(spot, hid, g0, xg2, xg3, g3, fg0, fxg2, fxg3, fg3)
    row_shapes = [array(rows // 2, full), array(count, full), array(3 * count, full)]

    def edge_weight(piece):
        tail = lax.dynamic_slice_in_dim(piece, width + line, 5, 1).astype(F32)
        return tail[:, :1] + tail[:, 4:]

    weights = [edge_weight(p) for p in (g0, xg2[:, full:], xg3[:, full:], g3)]

    def slot_sum(own_part, far_part, s, far_at, scaled):
        value = own_part[s * count : (s + 1) * count].astype(F32) + far_part[far_at * count : (far_at + 1) * count].astype(F32)
        return value * weights[s] if scaled else value

    def after(value, moving):
        return (value + moving.astype(F32)).astype(BF)

    def first_step(parts):
        return over_x(parts[0]), over_y(parts[2])

    def passed_on(parts, got):
        def add(a, b):
            return (a[1].astype(F32) + b[1].astype(F32)).astype(BF)

        return add(parts[1], got[0]), add(parts[3], got[1])

    def second_step(away):
        return over_y(away[0]), over_x(away[1])

    def totals(parts, got, last):
        def add(a, b, c):
            return a[0].astype(F32) + b[0].astype(F32) + c.astype(F32)

        return add(parts[1], got[0], last[0]), add(parts[3], got[1], last[1])

    down_got = first_step(down_parts)
    out_own, out_first, out_rest, pre_grad, *gate_parts = call(
        functools.partial(gate_grad_kernel, scale),
        [SMEM] + [ANY] * 28,
        [ANY] * 8,
        row_shapes + [array(rows, full)] + [array(2, PAD, units)] * 4,
        [held(units, full), held(rows, units), held(rows, full), held(rows, units), held(rows, units)]
        + [held(rows, full), held(rows, full), held(rows, full), held(full, units)]
        + [dma((16,)), dma((16,)), dma((8,)), dma((3,)), dma((4,)), dma((8,))],
        flops=LONG,
    )(spot, *weights_in, hid, grad, up_f, gate_f, *xs)
    *down_got, pre_grad, out_first, out_rest, gate_a, gate_b = together(
        *down_got, pre_grad, out_first, out_rest, gate_parts[0], gate_parts[2]
    )
    down_away = passed_on(down_parts, down_got)
    mix3 = slot_sum(out_own, over_core(out_first), 3, 0, True).astype(BF)
    m1 = backward(mix3)
    down_last = second_step(down_away)
    gate_got = over_x(gate_a), over_y(gate_b)
    out_rest = over_core(out_rest)
    in_own, in_first, in_rest, *up_parts = call(
        functools.partial(up_grad_kernel, scale),
        [SMEM] + [ANY] * 17,
        [ANY] * 7,
        row_shapes + [array(2, PAD, units)] * 4,
        [held(full, full), held(rows, full), held(rows, full), held(full, units), held(rows, full)]
        + [dma((8,)), dma((8,)), dma((4,)), dma((3,)), dma((8,))],
        flops=LONG,
    )(spot, *owns, *others, *xs, pre_grad)
    m2 = backward(after(slot_sum(out_own, out_rest, 2, 2, True), m1))
    g1, g2, l1, l2, m2, in_first, in_rest, up_a, up_b = together(
        *gate_got, *down_last, m2, in_first, in_rest, up_parts[0], up_parts[2]
    )
    gate_got, down_last = (g1, g2), (l1, l2)
    m3 = backward(after(slot_sum(out_own, out_rest, 1, 1, True), m2))
    gate_last = second_step(passed_on(gate_parts, gate_got))
    up_got = over_x(up_a), over_y(up_b)
    i1 = backward(slot_sum(in_own, over_core(in_first), 3, 0, False).astype(BF))
    in_rest = over_core(in_rest)

    def finish_rows(value, moving, spread):
        return call(functools.partial(finish_rows_kernel, spread), [VMEM] * 2, VMEM, array(width, count))(value, moving).T

    joined = jnp.concatenate(totals(down_parts, down_got, down_last), axis=0)[:, :width]
    grad_down = jnp.concatenate([joined[:MAIN], joined[164:176], joined[180:]], axis=0)
    u1, u2, l1, l2, m3, i1 = together(*up_got, *gate_last, m3, i1)
    up_got, gate_last = (u1, u2), (l1, l2)
    up_last = second_step(passed_on(up_parts, up_got))
    i2 = backward(after(slot_sum(in_own, in_rest, 2, 2, False), i1))
    mixed_out = finish_rows(slot_sum(out_own, out_rest, 0, 0, True), m3, False)
    i3 = backward(after(slot_sum(in_own, in_rest, 1, 1, False), i2))

    def split(parts, got, last):
        a, b = totals(parts, got, last)
        return jnp.where(core == 0, a, b), over_core(jnp.where(core == 0, b, a).astype(BF))

    gate_keep, gate_far = split(gate_parts, gate_got, gate_last)
    up_keep, up_far = split(up_parts, up_got, up_last)
    token_grad = finish_rows(slot_sum(in_own, in_rest, 0, 0, False), i3, True)
    grad_gate_up = call(
        finish_gate_up_kernel,
        [SMEM] + [VMEM] * 4,
        VMEM,
        jax.ShapeDtypeStruct((block, 2 * width), F32),
    )(spot, gate_keep, gate_far, up_keep, up_far)
    return (mixed_out, token_grad, grad_gate_up[None], grad_down[None])


def solution(mesh):
    placed = (
        P(("dp", "expert"), None),
        P(("dp", "expert"), None),
        P(("dp", "expert"), None),
        P(("dp", "expert"), None),
        P("expert", "dp", None),
        P("expert", "dp", None),
    )
    small = mesh.shape["dp"] == 8 and mesh.shape["expert"] == 4
    return jax.shard_map(
        paired if small else general,
        mesh=mesh,
        in_specs=placed,
        out_specs=(
            P(("dp", "expert"), None),
            P(("dp", "expert"), None),
            P("expert", "dp", None),
            P("expert", "dp", None),
        ),
        check_vma=False,
    )
```

```python
import functools
import math

import jax
import jax.numpy as jnp
from jax import lax
from jax.experimental import pallas as pl
from jax.experimental.pallas import tpu as pltpu
from jax.sharding import PartitionSpec as P

GLU_ALPHA = 1.702
BF = jnp.bfloat16
F32 = jnp.float32


def route_matrix(expert_ids, combine_weights, experts):
    hit = expert_ids[:, :, None] == jnp.arange(experts, dtype=jnp.int32)[None, None, :]
    return jnp.sum(jnp.where(hit, combine_weights[:, :, None], 0.0), axis=1)


def dense_forward(rows, weight_gu):
    half = weight_gu.shape[1] // 2
    pre = jnp.dot(rows, weight_gu, preferred_element_type=F32)
    gate, up = pre[:, :half], pre[:, half:]
    sig = jax.nn.sigmoid(GLU_ALPHA * gate)
    glu = gate * sig
    hidden = ((up + 1.0) * glu).astype(BF)
    gate_factor = (up + 1.0) * (sig + GLU_ALPHA * gate * sig * (1.0 - sig))
    return hidden, glu, gate_factor


def contract(left, right, dims):
    return lax.dot_general(left, right, ((dims[:1], dims[1:]), ((), ())), preferred_element_type=F32)


def general(tokens, expert_ids, combine_weights, out_grad, w_gate_up, w_down):
    experts = lax.axis_size("expert")
    replicas = lax.axis_size("dp")
    count, top = expert_ids.shape
    scale = 1.0 / math.sqrt(replicas * count * top)
    me = lax.axis_index("expert")
    table = route_matrix(expert_ids, combine_weights, experts)
    rows = lax.all_gather(tokens, "expert", axis=0, tiled=True)
    grads = lax.all_gather(out_grad, "expert", axis=0, tiled=True)
    table = lax.all_gather(table, "expert", axis=0, tiled=True)
    weight = lax.dynamic_slice_in_dim(table, me, 1, 1)
    row_grad = (weight * grads.astype(F32)).astype(BF)
    weight_gu = lax.all_gather(w_gate_up[0], "dp", axis=0, tiled=True)
    weight_down = lax.all_gather(w_down[0], "dp", axis=0, tiled=True)
    hidden, glu, gate_factor = dense_forward(rows, weight_gu)
    expert_out = jnp.dot(hidden, weight_down, preferred_element_type=F32).astype(BF)
    mixed = (weight * expert_out.astype(F32)).astype(BF)
    hidden_grad = contract(row_grad, weight_down, (1, 1))
    pre_grad = jnp.concatenate([hidden_grad * gate_factor, hidden_grad * glu], axis=1).astype(BF)
    input_grad = contract(pre_grad, weight_gu, (1, 1)).astype(BF)
    part_gu = (contract(rows, pre_grad, (0, 0)) * scale).astype(BF)
    part_down = (contract(hidden, row_grad, (0, 0)) * scale).astype(BF)

    def scatter(value, axis):
        return lax.psum_scatter(value, axis, scatter_dimension=0, tiled=True)

    return (
        scatter(mixed, "expert"),
        scatter(input_grad, "expert"),
        scatter(part_gu, "dp").astype(F32)[None],
        scatter(part_down, "dp").astype(F32)[None],
    )


PAD = 192
HALF = 96
MAIN = 156
LOT = 80
MIB = 1024 * 1024
LONG = 30_000_000_000


def zeros(shape, dtype=F32):
    return jnp.zeros(shape, dtype)


def prepare_kernel(spot, tokens_t, grads_t, ids_t, weights_t, w_gu, w_down, packed, own, other, high):
    core = spot[0]
    width, count = tokens_t.shape
    block = w_gu.shape[0]
    blocks = width // block
    gap = PAD - block
    full = blocks * PAD

    x = tokens_t[...].astype(F32)
    spread = []
    for i in range(blocks):
        spread += [x[i * block : (i + 1) * block], zeros((gap, count))]
    packed[:, :full] = jnp.concatenate(spread, axis=0).T.astype(BF)

    hit = [ids_t[...] == e for e in range(4)]
    table = jnp.concatenate(
        [jnp.sum(jnp.where(h, weights_t[...], 0.0), axis=0, keepdims=True) for h in hit], axis=0
    )
    coarse = table.astype(BF).astype(F32)
    rows = [grads_t[...].astype(F32), coarse, table - coarse, zeros((full - width - 8, count))]
    packed[:, full:] = jnp.concatenate(rows, axis=0).T.astype(BF)

    w = w_gu[...]
    lot = block - MAIN
    edge = zeros((block, lot // 3), BF)
    slim = zeros((block, lot // 6), BF)

    def half(parity):
        parts = []
        for j in range(blocks):
            at = (2 * j + parity) * block
            parts += [w[:, at : at + MAIN], edge, w[:, at + MAIN : at + MAIN + gap], slim, w[:, at + MAIN + gap : at + block]]
        return jnp.concatenate(parts, axis=1)

    even, odd = half(0), half(1)
    down = jnp.concatenate([w_down[...], zeros((block, full - width), BF)], axis=1)
    own[:block, :] = jnp.where(core == 0, even, odd)
    own[block:PAD, :] = down[MAIN : MAIN + gap]
    own[PAD:, :] = down[:LOT]
    other[...] = jnp.concatenate([jnp.where(core == 0, odd, even), zeros((gap, full), BF)], axis=0)
    high[...] = jnp.concatenate([down[LOT:MAIN], zeros((2 * LOT - MAIN, full), BF)], axis=0)


def join_kernel(other, high, w_down, out):
    block = w_down.shape[0]
    gap = PAD - block
    out[:PAD, :] = other[...]
    side = zeros((gap, out.shape[1] - w_down.shape[1]), BF)
    out[block:PAD, :] = jnp.concatenate([w_down[block - gap :, :], side], axis=1)
    out[PAD:, :] = high[...]


def start_all(copies):
    for c in copies:
        c.start()
    return copies


def wait_all(copies):
    for c in copies:
        c.wait()


def gate_up_copies(spot, owns, others, w_gu, sems):
    core, chip = spot[0], spot[1]
    copies = []
    for k in range(4):
        j = jnp.bitwise_xor(chip, k)
        for n, (ref, which) in enumerate(((owns[k], core), (others[k], 1 - core))):
            row = pl.multiple_of((2 * j + which) * PAD, PAD)
            copies.append(pltpu.make_async_copy(ref.at[pl.ds(0, PAD)], w_gu.at[pl.ds(row, PAD)], sems.at[2 * k + n]))
    return copies


def down_copies(spot, owns, others, w_down, sems):
    chip = spot[1]
    copies = []
    for k in range(4):
        base = jnp.bitwise_xor(chip, k) * PAD
        parts = (
            (owns[k].at[pl.ds(PAD, LOT)], 0, LOT),
            (others[k].at[pl.ds(PAD, LOT)], LOT, LOT),
            (owns[k].at[pl.ds(PAD - 16, 16)], 2 * LOT, 16),
            (others[k].at[pl.ds(PAD - 16, 16)], 2 * LOT + 16, 16),
        )
        for ref, at, size in parts:
            row = pl.multiple_of(base + at, 16)
            copies.append(pltpu.make_async_copy(ref, w_down.at[pl.ds(row, size)], sems.at[len(copies)]))
    return copies


def row_copies(pieces, starts, scratch, sems):
    count, wide = pieces[0].shape[0], scratch.shape[1]
    return [
        pltpu.make_async_copy(p.at[:, pl.ds(start, wide)], scratch.at[pl.ds(n * count, count)], sems.at[n])
        for n, (p, start) in enumerate(zip(pieces, starts))
    ]


def chunk_copies(source, target, step, sems, base=0):
    return [
        pltpu.make_async_copy(source.at[pl.ds(m, step)], target.at[pl.ds(m, step)], sems.at[base + m // step])
        for m in range(0, source.shape[0], step)
    ]


STEP = 256
X_AT = (0,) * 8
G_AT = (8 * PAD,) * 8


def scatter_copies(chip, part, stride, a_at, b_at, send_a, keep_a, send_b, keep_b, sems, first=0):
    size = send_a.shape[1]
    copies = []
    plan_a = ((1, send_a, first), (3, send_a, first + 1), (0, keep_a, 0), (2, keep_a, 1))
    plan_b = ((2, send_b, first), (3, send_b, first + 1), (0, keep_b, 0), (1, keep_b, 1))
    for at, plan in ((a_at, plan_a), (b_at, plan_b)):
        for rel, ref, slot in plan:
            row = jnp.bitwise_xor(chip, rel) * (stride * PAD) + at
            source = part.at[pl.ds(pl.multiple_of(row, HALF), size)]
            copies.append(pltpu.make_async_copy(source, ref.at[slot], sems.at[len(copies)]))
    return copies


def forward_kernel(scale, *refs):
    spot, owns, others, pieces = refs[0], refs[1:5], refs[5:9], refs[9:17]
    up_out, gate_out, grad_out, out_own, out_first, out_rest, *parts = refs[17:27]
    w_gu, w_down, x, g, hid, up_f, gate_f, wide, out, part = refs[27:37]
    w_sems, down_sems, x_sems, g_sems, out_sems, row_sems, part_sems = refs[37:]
    line, chip = spot[2], spot[1]
    gu = start_all(gate_up_copies(spot, owns, others, w_gu, w_sems))
    xs = row_copies(pieces, X_AT, x, x_sems)
    gs = row_copies(pieces, G_AT, g, g_sems)
    per = STEP // pieces[0].shape[0]
    start_all(xs[:per])
    wait_all(gu)
    start_all(xs[per:])
    start_all(gs)
    down = start_all(down_copies(spot, owns, others, w_down, down_sems))
    half = w_gu.shape[1] // 2
    full = g.shape[1]
    lane = lax.broadcasted_iota(jnp.int32, (STEP, 128), 1)
    picked = (lane == 32 + line) | (lane == 36 + line)
    outs = [
        chunk_copies(a, b, STEP, out_sems, base) for a, b, base in ((up_f, up_out, 0), (gate_f, gate_out, 4), (g, grad_out, 8))
    ]
    for n in range(x.shape[0] // STEP):
        at = pl.ds(n * STEP, STEP)
        wait_all(xs[n * per : (n + 1) * per])
        pre = jnp.dot(x[at, :], w_gu[...], preferred_element_type=F32)
        gate, up = pre[:, :half], pre[:, half:] + 1.0
        sig = jax.nn.sigmoid(GLU_ALPHA * gate)
        glu = gate * sig
        hid[at, :] = (up * glu).astype(BF)
        up_f[at, :] = glu.astype(BF)
        gate_f[at, :] = (up * (sig + GLU_ALPHA * glu * (1.0 - sig))).astype(BF)
        wait_all(gs[n * per : (n + 1) * per])
        edge = g[at, pl.ds(full - 128, 128)].astype(F32)
        weight = jnp.sum(jnp.where(picked, edge, 0.0), axis=1, keepdims=True)
        g[at, :] = (weight * g[at, :].astype(F32)).astype(BF)
        wide[at, :] = jnp.broadcast_to(weight, (STEP, 128))
        for group in outs:
            group[n].start()
    for m in range(0, part.shape[0], STEP):
        at = pl.ds(m, STEP)
        part[at, :] = (contract(hid[:, at], g[...], (0, 0)) * scale).astype(BF)
    sent = start_all(scatter_copies(chip, part, 1, 0, HALF, *parts, part_sems))
    wait_all(down)
    rows = row_outs(out, out_own, out_first, out_rest, row_sems)
    for n in (3, 2, 1, 0):
        at = pl.ds(n * STEP, STEP)
        part_out = jnp.dot(hid[at, :], w_down[...], preferred_element_type=F32)
        out[at, :] = (part_out * wide[at, :1]).astype(BF)
    start_all(rows)
    for group in outs:
        wait_all(group)
    wait_all(sent)
    wait_all(rows)


def row_outs(out, own, first, rest, sems):
    last = out.shape[0] // 8
    return [
        pltpu.make_async_copy(out.at[pl.ds(7 * last, last)], first, sems.at[0]),
        pltpu.make_async_copy(out.at[pl.ds(4 * last, 3 * last)], rest, sems.at[1]),
        pltpu.make_async_copy(out.at[pl.ds(0, 4 * last)], own, sems.at[2]),
    ]


def gate_grad_kernel(scale, *refs):
    spot, owns, others = refs[0], refs[1:5], refs[5:9]
    grad_in, up_in, gate_in, pieces = refs[9], refs[10], refs[11], refs[12:20]
    pre_out, *parts = refs[20:25]
    w_down, g, up_f, gate_f, pre_grad, x, part, w_sems, in_sems, x_sems, out_sems, part_sems = refs[25:]
    down = start_all(down_copies(spot, owns, others, w_down, w_sems))
    loads = [
        chunk_copies(a, b, STEP, in_sems, base) for a, b, base in ((grad_in, g, 0), (up_in, up_f, 4), (gate_in, gate_f, 8))
    ]
    xs = row_copies(pieces, X_AT, x, x_sems)
    groups = list(zip(*loads))
    start_all(groups[0])
    wait_all(down)
    for group in groups[1:]:
        start_all(group)
    half = w_down.shape[0]
    pres = chunk_copies(pre_grad, pre_out, STEP, out_sems)
    for n, group in enumerate(groups):
        at = pl.ds(n * STEP, STEP)
        wait_all(group)
        if n == 1:
            start_all(xs)
        hidden_grad = contract(g[at, :], w_down[...], (1, 1))
        pre_grad[at, :half] = (hidden_grad * gate_f[at, :].astype(F32)).astype(BF)
        pre_grad[at, half:] = (hidden_grad * up_f[at, :].astype(F32)).astype(BF)
        pres[n].start()
    wait_all(xs)
    for m in range(0, part.shape[0], 2 * PAD):
        at = pl.ds(m, 2 * PAD)
        part[at, :] = (contract(x[:, at], pre_grad[:, :half], (0, 0)) * scale).astype(BF)
    outs = start_all(scatter_copies(spot[1], part, 2, 0, PAD, *parts, part_sems))
    wait_all(pres)
    wait_all(outs)


def up_grad_kernel(scale, *refs):
    spot, owns, others, pieces, pre_in = refs[0], refs[1:5], refs[5:9], refs[9:17], refs[17]
    in_own, in_first, in_rest, *parts = refs[18:25]
    w_gu, x, pre_grad, part, out, w_sems, x_sems, in_sems, out_sems, part_sems = refs[25:]
    loads = start_all(chunk_copies(pre_in, pre_grad, STEP, in_sems))
    xs = start_all(row_copies(pieces, X_AT, x, x_sems))
    wait_all(loads)
    wait_all(xs)
    gu = start_all(gate_up_copies(spot, owns, others, w_gu, w_sems))
    half = part.shape[1]
    for m in range(0, part.shape[0], 2 * PAD):
        at = pl.ds(m, 2 * PAD)
        part[at, :] = (contract(x[:, at], pre_grad[:, half:], (0, 0)) * scale).astype(BF)
    outs = start_all(scatter_copies(spot[1], part, 2, 0, PAD, *parts, part_sems, first=1))
    wait_all(gu)
    rows = row_outs(out, in_own, in_first, in_rest, out_sems)
    for n in (3, 2, 1, 0):
        at = pl.ds(n * STEP, STEP)
        out[at, :] = contract(pre_grad[at, :], w_gu[...], (1, 1)).astype(BF)
    start_all(rows)
    wait_all(outs)
    wait_all(rows)


def pass_kernel(keep_a, got_a, keep_b, got_b, up_a, up_b, out_a, out_b, ins, sums, in_sems, out_sems):
    loads = [
        pltpu.make_async_copy(ref.at[1], ins.at[n], in_sems.at[n]) for n, ref in enumerate((keep_a, got_a, keep_b, got_b))
    ]
    start_all(loads)
    wait_all(loads)
    for n in range(2):
        sums[n] = (ins[2 * n].astype(F32) + ins[2 * n + 1].astype(F32)).astype(BF)
    stores = [pltpu.make_async_copy(sums.at[n], ref.at[0], out_sems.at[n]) for n, ref in enumerate((out_b, out_a))]
    start_all(stores)
    wait_all(stores)


def finish_rows_kernel(spread, keep, got, out_t):
    width = out_t.shape[0]
    total = (keep[...].astype(F32) + got[...].astype(F32)).T
    if spread:
        block = width // 8
        total = jnp.concatenate([total[i * PAD : i * PAD + block] for i in range(8)], axis=0)
    out_t[...] = total[:width].astype(BF)


def finish_gate_up_kernel(spot, gate_keep, gate_far, up_keep, up_far, out):
    core = spot[0]
    block = out.shape[0]
    parts = []
    for keep, far in ((gate_keep, gate_far), (up_keep, up_far)):
        mine = keep[...].astype(F32)[:block]
        theirs = far[...].astype(F32)[:block]
        even = jnp.where(core == 0, mine, theirs)
        odd = jnp.where(core == 0, theirs, mine)
        for j in range(4):
            for p in (even, odd):
                at = j * PAD
                parts += [p[:, at : at + MAIN], p[:, at + 164 : at + 176], p[:, at + 180 : at + PAD]]
    out[...] = jnp.concatenate(parts, axis=1).reshape(out.shape)


def finish_down_kernel(keep_a, got_a, last_a, keep_b, got_b, last_b, out):
    def total(keep, got, last):
        return keep[0].astype(F32) + got[0].astype(F32) + last[...].astype(F32)

    rows = jnp.concatenate([total(keep_a, got_a, last_a), total(keep_b, got_b, last_b)], axis=0)
    rows = jnp.concatenate([rows[:MAIN], rows[164:176], rows[180:]], axis=0)
    out[...] = rows[:, : out.shape[2]].reshape(out.shape)


VMEM = pl.BlockSpec(memory_space=pltpu.VMEM)
SMEM = pl.BlockSpec(memory_space=pltpu.SMEM)
ANY = pl.BlockSpec(memory_space=pl.ANY)


def call(body, in_specs, out_specs, out_shape, scratch=(), mib=58, flops=1000, aliases=None):
    return pl.pallas_call(
        body,
        in_specs=in_specs,
        out_specs=out_specs,
        out_shape=out_shape,
        scratch_shapes=list(scratch),
        input_output_aliases=aliases or {},
        compiler_params=pltpu.CompilerParams(vmem_limit_bytes=mib * MIB),
        cost_estimate=pl.CostEstimate(flops=flops, bytes_accessed=1000, transcendentals=0),
    )


def paired(tokens, expert_ids, combine_weights, out_grad, w_gate_up, w_down):
    count, top = expert_ids.shape
    width = tokens.shape[1]
    scale = 1.0 / math.sqrt(8 * count * top)
    place = lax.axis_index("dp")
    line = lax.axis_index("expert")
    core = place % 2
    spot = jnp.stack([core, place // 2, line]).astype(jnp.int32)
    block = w_gate_up.shape[1]
    full = 8 * PAD
    units = 4 * PAD
    rows = 8 * count
    dma = pltpu.SemaphoreType.DMA

    def swap(bit):
        pairs = [(i, i ^ bit) for i in range(8)]
        return lambda value: lax.ppermute(value, "dp", pairs)

    over_core, over_x, over_y = swap(1), swap(2), swap(4)

    def onward(value):
        return lax.ppermute(value, "expert", [(i, (i + 1) % 4) for i in range(4)])

    def backward(value):
        return lax.ppermute(value, "expert", [(i, (i + 3) % 4) for i in range(4)])

    def array(*shape):
        return jax.ShapeDtypeStruct(shape, BF)

    def held(*shape):
        return pltpu.VMEM(shape, BF)

    def together(*values):
        return lax.optimization_barrier(values)

    xg0, own, other, high = call(
        prepare_kernel,
        [SMEM] + [VMEM] * 6,
        [VMEM] * 4,
        [array(count, 2 * full), array(PAD + LOT, full), array(PAD, full), array(LOT, full)],
    )(spot, tokens.T, out_grad.T, expert_ids.T, combine_weights.T, w_gate_up[0], w_down[0])

    other, own_x, own_y, xg1, fxg0 = over_core(other), over_x(own), over_y(own), onward(xg0), over_core(xg0)
    other = call(join_kernel, [VMEM] * 3, VMEM, array(PAD + LOT, full))(other, high, w_down[0])
    own_x, own_y, xg1, other, fxg0 = together(own_x, own_y, xg1, other, fxg0)
    other_x, other_y, xg2, fxg1 = over_x(other), over_y(other), onward(xg1), over_core(xg1)
    other_x, other_y, xg2, fxg1, own_x = together(other_x, other_y, xg2, fxg1, own_x)
    own_xy, other_xy, xg3, fxg2 = over_y(own_x), over_x(other_y), onward(xg2), over_core(xg2)
    fxg3 = over_core(xg3)

    owns = (own, own_x, own_y, own_xy)
    others = (other, other_x, other_y, other_xy)
    xs = (xg0, xg1, xg2, xg3, fxg0, fxg1, fxg2, fxg3)
    row_shapes = [array(rows // 2, full), array(count, full), array(3 * count, full)]
    up_f, gate_f, grad, out_own, out_first, out_rest, *down_parts = call(
        functools.partial(forward_kernel, scale),
        [SMEM] + [ANY] * 16,
        [ANY] * 10,
        [array(rows, units)] * 2 + [array(rows, full)] + row_shapes + [array(2, HALF, full)] * 4,
        [held(full, full), held(units, full), held(rows, full), held(rows, full)]
        + [held(rows, units)] * 3
        + [pltpu.VMEM((rows, 128), F32), held(rows, full), held(units, full)]
        + [dma((8,)), dma((16,)), dma((8,)), dma((8,)), dma((12,)), dma((3,)), dma((8,))],
        flops=LONG,
    )(spot, *owns, *others, *xs)

    def slot_sum(own_part, far_part, s, far):
        return own_part[s * count : (s + 1) * count].astype(F32) + far_part[far * count : (far + 1) * count].astype(F32)

    def after(value, moving):
        return (value + moving.astype(F32)).astype(BF)

    def first_step(parts):
        return over_x(parts[0]), over_y(parts[2])

    def passed_on(parts, got):
        def add(a, b):
            return (a[1].astype(F32) + b[1].astype(F32)).astype(BF)

        return add(parts[1], got[0]), add(parts[3], got[1])

    def second_step(away):
        return over_y(away[0]), over_x(away[1])

    def totals(parts, got, last):
        def add(a, b, c):
            return a[0].astype(F32) + b[0].astype(F32) + c.astype(F32)

        return add(parts[1], got[0], last[0]), add(parts[3], got[1], last[1])

    down_got = first_step(down_parts)
    m1 = slot_sum(out_own, over_core(out_first), 3, 0).astype(BF)
    m1, grad = together(m1, grad)
    m1 = backward(m1)
    out_rest = over_core(out_rest)
    pre_grad, *gate_parts = call(
        functools.partial(gate_grad_kernel, scale),
        [SMEM] + [ANY] * 19,
        [ANY] * 5,
        [array(rows, full)] + [array(2, PAD, units)] * 4,
        [held(units, full), held(rows, full), held(rows, units), held(rows, units), held(rows, full)]
        + [held(rows, full), held(full, units), dma((16,)), dma((12,)), dma((8,)), dma((4,)), dma((8,))],
        flops=LONG,
    )(spot, *owns, *others, grad, up_f, gate_f, *xs)
    *down_got, m1, pre_grad, gate_a, gate_b, out_rest = together(
        *down_got, m1, pre_grad, gate_parts[0], gate_parts[2], out_rest
    )
    m2 = backward(after(slot_sum(out_own, out_rest, 2, 2), m1))
    down_last = second_step(passed_on(down_parts, down_got))
    gate_got = over_x(gate_a), over_y(gate_b)
    in_own, in_first, in_rest, *up_parts = call(
        functools.partial(up_grad_kernel, scale),
        [SMEM] + [ANY] * 17,
        [ANY] * 7,
        row_shapes + [array(3, PAD, units), array(2, PAD, units)] * 2,
        [held(full, full), held(rows, full), held(rows, full), held(full, units), held(rows, full)]
        + [dma((8,)), dma((8,)), dma((4,)), dma((4,)), dma((8,))],
        flops=LONG,
    )(spot, *owns, *others, *xs, pre_grad)
    m2, in_first, in_rest, l1, l2, g1, g2, up_a, up_b = together(
        m2, in_first, in_rest, *down_last, *gate_got, up_parts[0], up_parts[2]
    )
    down_last, gate_got = (l1, l2), (g1, g2)
    m3 = after(slot_sum(out_own, out_rest, 1, 1), m2)
    up_a, up_b = call(
        pass_kernel,
        [ANY] * 6,
        [ANY] * 2,
        [array(3, PAD, units)] * 2,
        [held(4, PAD, units), held(2, PAD, units), dma((4,)), dma((2,))],
        aliases={4: 0, 5: 1},
    )(gate_parts[1], gate_got[0], gate_parts[3], gate_got[1], up_a, up_b)
    up_a, up_b, m3, in_first, in_rest = together(up_a, up_b, m3, in_first, in_rest)
    by_y, by_x, m3 = over_y(up_b), over_x(up_a), backward(m3)
    i1 = backward(slot_sum(in_own, over_core(in_first), 3, 0).astype(BF))
    in_rest = over_core(in_rest)

    def finish_rows(value, moving, spread):
        return call(functools.partial(finish_rows_kernel, spread), [VMEM] * 2, VMEM, array(width, count))(value, moving).T

    grad_down = call(
        finish_down_kernel, [VMEM] * 6, VMEM, jax.ShapeDtypeStruct((block, 1, width), F32)
    )(down_parts[1], down_got[0], down_last[0], down_parts[3], down_got[1], down_last[1])
    by_x, by_y, m3, grad_down = together(by_x, by_y, m3, grad_down)
    up_got, gate_last = (by_x[1:], by_y[1:]), (by_y[0], by_x[0])
    i2 = backward(after(slot_sum(in_own, in_rest, 2, 2), i1))
    up_last = second_step(passed_on(up_parts, up_got))

    def split(parts, got, last):
        a, b = totals(parts, got, last)
        return jnp.where(core == 0, a, b), over_core(jnp.where(core == 0, b, a).astype(BF))

    gate_keep, gate_far = split(gate_parts, gate_got, gate_last)
    i3 = after(slot_sum(in_own, in_rest, 1, 1), i2)
    mixed_out = finish_rows(slot_sum(out_own, out_rest, 0, 0), m3, False)
    l1, l2, gate_keep, gate_far, mixed_out, _ = together(*up_last, gate_keep, gate_far, mixed_out, i3)
    i3 = backward(i3)
    up_keep, up_far = split(up_parts, up_got, (l1, l2))
    grad_gate_up = call(
        finish_gate_up_kernel,
        [SMEM] + [VMEM] * 4,
        VMEM,
        jax.ShapeDtypeStruct((block, 1, 2 * width), F32),
    )(spot, gate_keep, gate_far, up_keep, up_far)
    token_grad = finish_rows(slot_sum(in_own, in_rest, 0, 0), i3, True)
    return (mixed_out, token_grad, grad_gate_up.transpose(1, 0, 2), grad_down.transpose(1, 0, 2))


def solution(mesh):
    placed = (
        P(("dp", "expert"), None),
        P(("dp", "expert"), None),
        P(("dp", "expert"), None),
        P(("dp", "expert"), None),
        P("expert", "dp", None),
        P("expert", "dp", None),
    )
    small = mesh.shape["dp"] == 8 and mesh.shape["expert"] == 4
    return jax.shard_map(
        paired if small else general,
        mesh=mesh,
        in_specs=placed,
        out_specs=(
            P(("dp", "expert"), None),
            P(("dp", "expert"), None),
            P("expert", "dp", None),
            P("expert", "dp", None),
        ),
        check_vma=False,
    )
```

```python
import functools
import math

import jax
import jax.numpy as jnp
from jax import lax
from jax.experimental import pallas as pl
from jax.experimental.pallas import tpu as pltpu
from jax.sharding import PartitionSpec as P

GLU_ALPHA = 1.702
BF = jnp.bfloat16
F32 = jnp.float32


def route_matrix(expert_ids, combine_weights, experts):
    hit = expert_ids[:, :, None] == jnp.arange(experts, dtype=jnp.int32)[None, None, :]
    return jnp.sum(jnp.where(hit, combine_weights[:, :, None], 0.0), axis=1)


def dense_forward(rows, weight_gu):
    half = weight_gu.shape[1] // 2
    pre = jnp.dot(rows, weight_gu, preferred_element_type=F32)
    gate, up = pre[:, :half], pre[:, half:]
    sig = jax.nn.sigmoid(GLU_ALPHA * gate)
    glu = gate * sig
    hidden = ((up + 1.0) * glu).astype(BF)
    gate_factor = (up + 1.0) * (sig + GLU_ALPHA * gate * sig * (1.0 - sig))
    return hidden, glu, gate_factor


def contract(left, right, dims):
    return lax.dot_general(left, right, ((dims[:1], dims[1:]), ((), ())), preferred_element_type=F32)


def general(tokens, expert_ids, combine_weights, out_grad, w_gate_up, w_down):
    experts = lax.axis_size("expert")
    replicas = lax.axis_size("dp")
    count, top = expert_ids.shape
    scale = 1.0 / math.sqrt(replicas * count * top)
    me = lax.axis_index("expert")
    table = route_matrix(expert_ids, combine_weights, experts)
    rows = lax.all_gather(tokens, "expert", axis=0, tiled=True)
    grads = lax.all_gather(out_grad, "expert", axis=0, tiled=True)
    table = lax.all_gather(table, "expert", axis=0, tiled=True)
    weight = lax.dynamic_slice_in_dim(table, me, 1, 1)
    row_grad = (weight * grads.astype(F32)).astype(BF)
    weight_gu = lax.all_gather(w_gate_up[0], "dp", axis=0, tiled=True)
    weight_down = lax.all_gather(w_down[0], "dp", axis=0, tiled=True)
    hidden, glu, gate_factor = dense_forward(rows, weight_gu)
    expert_out = jnp.dot(hidden, weight_down, preferred_element_type=F32).astype(BF)
    mixed = (weight * expert_out.astype(F32)).astype(BF)
    hidden_grad = contract(row_grad, weight_down, (1, 1))
    pre_grad = jnp.concatenate([hidden_grad * gate_factor, hidden_grad * glu], axis=1).astype(BF)
    input_grad = contract(pre_grad, weight_gu, (1, 1)).astype(BF)
    part_gu = (contract(rows, pre_grad, (0, 0)) * scale).astype(BF)
    part_down = (contract(hidden, row_grad, (0, 0)) * scale).astype(BF)

    def scatter(value, axis):
        return lax.psum_scatter(value, axis, scatter_dimension=0, tiled=True)

    return (
        scatter(mixed, "expert"),
        scatter(input_grad, "expert"),
        scatter(part_gu, "dp").astype(F32)[None],
        scatter(part_down, "dp").astype(F32)[None],
    )


PAD = 192
HALF = 96
MAIN = 156
LOT = 80
MIB = 1024 * 1024
LONG = 30_000_000_000


def zeros(shape, dtype=F32):
    return jnp.zeros(shape, dtype)


def prepare_rows_kernel(tokens_t, grads_t, ids_t, weights_t, packed):
    width, count = tokens_t.shape
    blocks = 8
    block = width // blocks
    full = blocks * PAD
    x = tokens_t[...].astype(F32)
    spread = []
    for i in range(blocks):
        spread += [x[i * block : (i + 1) * block], zeros((PAD - block, count))]
    packed[:, :full] = jnp.concatenate(spread, axis=0).T.astype(BF)

    hit = [ids_t[...] == e for e in range(4)]
    table = jnp.concatenate(
        [jnp.sum(jnp.where(h, weights_t[...], 0.0), axis=0, keepdims=True) for h in hit], axis=0
    )
    coarse = table.astype(BF).astype(F32)
    rows = [grads_t[...].astype(F32), coarse, table - coarse, zeros((full - width - 8, count))]
    packed[:, full:] = jnp.concatenate(rows, axis=0).T.astype(BF)


def prepare_weights_kernel(spot, w_gu, w_down, own, other, high):
    core = spot[0]
    block, width = w_down.shape
    blocks = width // block
    gap = PAD - block
    full = blocks * PAD
    w = w_gu[...]
    lot = block - MAIN
    edge = zeros((block, lot // 3), BF)
    slim = zeros((block, lot // 6), BF)

    def half(parity):
        parts = []
        for j in range(blocks):
            at = (2 * j + parity) * block
            parts += [w[:, at : at + MAIN], edge, w[:, at + MAIN : at + MAIN + gap], slim, w[:, at + MAIN + gap : at + block]]
        return jnp.concatenate(parts, axis=1)

    even, odd = half(0), half(1)
    down = jnp.concatenate([w_down[...], zeros((block, full - width), BF)], axis=1)
    own[:block, :] = jnp.where(core == 0, even, odd)
    own[block:PAD, :] = down[MAIN : MAIN + gap]
    own[PAD:, :] = down[:LOT]
    other[...] = jnp.concatenate([jnp.where(core == 0, odd, even), zeros((gap, full), BF)], axis=0)
    high[...] = jnp.concatenate([down[LOT:MAIN], zeros((2 * LOT - MAIN, full), BF)], axis=0)


def join_kernel(other, high, w_down, out):
    block = w_down.shape[0]
    gap = PAD - block
    out[:PAD, :] = other[...]
    side = zeros((gap, out.shape[1] - w_down.shape[1]), BF)
    out[block:PAD, :] = jnp.concatenate([w_down[block - gap :, :], side], axis=1)
    out[PAD:, :] = high[...]


def start_all(copies):
    for c in copies:
        c.start()
    return copies


def wait_all(copies):
    for c in copies:
        c.wait()


def gate_up_copies(spot, owns, others, w_gu, sems):
    core, chip = spot[0], spot[1]
    copies = []
    for k in range(4):
        j = jnp.bitwise_xor(chip, k)
        for n, (ref, which) in enumerate(((owns[k], core), (others[k], 1 - core))):
            row = pl.multiple_of((2 * j + which) * PAD, PAD)
            copies.append(pltpu.make_async_copy(ref.at[pl.ds(0, PAD)], w_gu.at[pl.ds(row, PAD)], sems.at[2 * k + n]))
    return copies


def down_copies(spot, owns, others, w_down, sems):
    chip = spot[1]
    copies = []
    for k in range(4):
        base = jnp.bitwise_xor(chip, k) * PAD
        parts = (
            (owns[k].at[pl.ds(PAD, LOT)], 0, LOT),
            (others[k].at[pl.ds(PAD, LOT)], LOT, LOT),
            (owns[k].at[pl.ds(PAD - 16, 16)], 2 * LOT, 16),
            (others[k].at[pl.ds(PAD - 16, 16)], 2 * LOT + 16, 16),
        )
        for ref, at, size in parts:
            row = pl.multiple_of(base + at, 16)
            copies.append(pltpu.make_async_copy(ref, w_down.at[pl.ds(row, size)], sems.at[len(copies)]))
    return copies


def row_copies(pieces, starts, scratch, sems):
    count, wide = pieces[0].shape[0], scratch.shape[1]
    return [
        pltpu.make_async_copy(p.at[:, pl.ds(start, wide)], scratch.at[pl.ds(n * count, count)], sems.at[n])
        for n, (p, start) in enumerate(zip(pieces, starts))
    ]


def chunk_copies(source, target, step, sems, base=0):
    return [
        pltpu.make_async_copy(source.at[pl.ds(m, step)], target.at[pl.ds(m, step)], sems.at[base + m // step])
        for m in range(0, source.shape[0], step)
    ]


STEP = 256
X_AT = (0,) * 8
G_AT = (8 * PAD,) * 8


def scatter_copies(chip, part, stride, a_at, b_at, send_a, keep_a, send_b, keep_b, sems, first=0):
    size = send_a.shape[1]
    copies = []
    plan_a = ((1, send_a, first), (3, send_a, first + 1), (0, keep_a, 0), (2, keep_a, 1))
    plan_b = ((2, send_b, first), (3, send_b, first + 1), (0, keep_b, 0), (1, keep_b, 1))
    for at, plan in ((a_at, plan_a), (b_at, plan_b)):
        for rel, ref, slot in plan:
            row = jnp.bitwise_xor(chip, rel) * (stride * PAD) + at
            source = part.at[pl.ds(pl.multiple_of(row, HALF), size)]
            copies.append(pltpu.make_async_copy(source, ref.at[slot], sems.at[len(copies)]))
    return copies


def forward_kernel(scale, *refs):
    spot, owns, others, pieces = refs[0], refs[1:5], refs[5:9], refs[9:17]
    up_out, gate_out, grad_out, out_own, out_first, out_rest, *parts = refs[17:27]
    w_gu, w_down, x, g, hid, up_f, gate_f, wide, out, part = refs[27:37]
    w_sems, down_sems, x_sems, g_sems, out_sems, row_sems, part_sems = refs[37:]
    line, chip = spot[2], spot[1]
    gu = start_all(gate_up_copies(spot, owns, others, w_gu, w_sems))
    xs = row_copies(pieces, X_AT, x, x_sems)
    gs = row_copies(pieces, G_AT, g, g_sems)
    per = STEP // pieces[0].shape[0]
    start_all(xs[:per])
    wait_all(gu)
    start_all(xs[per:])
    start_all(gs)
    down = start_all(down_copies(spot, owns, others, w_down, down_sems))
    half = w_gu.shape[1] // 2
    full = g.shape[1]
    lane = lax.broadcasted_iota(jnp.int32, (STEP, 128), 1)
    picked = (lane == 32 + line) | (lane == 36 + line)
    outs = [
        chunk_copies(a, b, STEP, out_sems, base) for a, b, base in ((up_f, up_out, 0), (gate_f, gate_out, 4), (g, grad_out, 8))
    ]
    for n in range(x.shape[0] // STEP):
        at = pl.ds(n * STEP, STEP)
        wait_all(xs[n * per : (n + 1) * per])
        pre = jnp.dot(x[at, :], w_gu[...], preferred_element_type=F32)
        gate, up = pre[:, :half], pre[:, half:] + 1.0
        sig = jax.nn.sigmoid(GLU_ALPHA * gate)
        glu = gate * sig
        hid[at, :] = (up * glu).astype(BF)
        up_f[at, :] = glu.astype(BF)
        gate_f[at, :] = (up * (sig + GLU_ALPHA * glu * (1.0 - sig))).astype(BF)
        wait_all(gs[n * per : (n + 1) * per])
        edge = g[at, pl.ds(full - 128, 128)].astype(F32)
        weight = jnp.sum(jnp.where(picked, edge, 0.0), axis=1, keepdims=True)
        g[at, :] = (weight * g[at, :].astype(F32)).astype(BF)
        wide[at, :] = jnp.broadcast_to(weight, (STEP, 128))
        for group in outs:
            group[n].start()
    for m in range(0, part.shape[0], STEP):
        at = pl.ds(m, STEP)
        part[at, :] = (contract(hid[:, at], g[...], (0, 0)) * scale).astype(BF)
    sent = start_all(scatter_copies(chip, part, 1, 0, HALF, *parts, part_sems))
    wait_all(down)
    rows = row_outs(out, out_own, out_first, out_rest, row_sems)
    for n in (3, 2, 1, 0):
        at = pl.ds(n * STEP, STEP)
        part_out = jnp.dot(hid[at, :], w_down[...], preferred_element_type=F32)
        out[at, :] = (part_out * wide[at, :1]).astype(BF)
    start_all(rows)
    for group in outs:
        wait_all(group)
    wait_all(sent)
    wait_all(rows)


def row_outs(out, own, first, rest, sems):
    last = out.shape[0] // 8
    return [
        pltpu.make_async_copy(out.at[pl.ds(7 * last, last)], first, sems.at[0]),
        pltpu.make_async_copy(out.at[pl.ds(4 * last, 3 * last)], rest, sems.at[1]),
        pltpu.make_async_copy(out.at[pl.ds(0, 4 * last)], own, sems.at[2]),
    ]


def gate_grad_kernel(scale, *refs):
    spot, owns, others = refs[0], refs[1:5], refs[5:9]
    grad_in, up_in, gate_in, pieces = refs[9], refs[10], refs[11], refs[12:20]
    pre_out, *parts = refs[20:25]
    w_down, g, up_f, gate_f, pre_grad, x, part, w_sems, in_sems, x_sems, out_sems, part_sems = refs[25:]
    down = start_all(down_copies(spot, owns, others, w_down, w_sems))
    loads = [
        chunk_copies(a, b, STEP, in_sems, base) for a, b, base in ((grad_in, g, 0), (up_in, up_f, 4), (gate_in, gate_f, 8))
    ]
    xs = row_copies(pieces, X_AT, x, x_sems)
    groups = list(zip(*loads))
    start_all(groups[0])
    wait_all(down)
    for group in groups[1:]:
        start_all(group)
    half = w_down.shape[0]
    pres = chunk_copies(pre_grad, pre_out, STEP, out_sems)
    for n, group in enumerate(groups):
        at = pl.ds(n * STEP, STEP)
        wait_all(group)
        if n == 1:
            start_all(xs)
        hidden_grad = contract(g[at, :], w_down[...], (1, 1))
        pre_grad[at, :half] = (hidden_grad * gate_f[at, :].astype(F32)).astype(BF)
        pre_grad[at, half:] = (hidden_grad * up_f[at, :].astype(F32)).astype(BF)
        pres[n].start()
    wait_all(xs)
    for m in range(0, part.shape[0], 2 * PAD):
        at = pl.ds(m, 2 * PAD)
        part[at, :] = (contract(x[:, at], pre_grad[:, :half], (0, 0)) * scale).astype(BF)
    outs = start_all(scatter_copies(spot[1], part, 2, 0, PAD, *parts, part_sems))
    wait_all(pres)
    wait_all(outs)


def up_grad_kernel(scale, *refs):
    spot, owns, others, pieces, pre_in = refs[0], refs[1:5], refs[5:9], refs[9:17], refs[17]
    in_own, in_first, in_rest, *parts = refs[18:25]
    w_gu, x, pre_grad, part, out, w_sems, x_sems, in_sems, out_sems, part_sems = refs[25:]
    loads = start_all(chunk_copies(pre_in, pre_grad, STEP, in_sems))
    xs = start_all(row_copies(pieces, X_AT, x, x_sems))
    wait_all(loads)
    wait_all(xs)
    gu = start_all(gate_up_copies(spot, owns, others, w_gu, w_sems))
    half = part.shape[1]
    for m in range(0, part.shape[0], 2 * PAD):
        at = pl.ds(m, 2 * PAD)
        part[at, :] = (contract(x[:, at], pre_grad[:, half:], (0, 0)) * scale).astype(BF)
    outs = start_all(scatter_copies(spot[1], part, 2, 0, PAD, *parts, part_sems, first=1))
    wait_all(gu)
    rows = row_outs(out, in_own, in_first, in_rest, out_sems)
    for n in (3, 2, 1, 0):
        at = pl.ds(n * STEP, STEP)
        out[at, :] = contract(pre_grad[at, :], w_gu[...], (1, 1)).astype(BF)
    start_all(rows)
    wait_all(outs)
    wait_all(rows)


def pass_kernel(keep_a, got_a, keep_b, got_b, up_a, up_b, out_a, out_b, ins, sums, in_sems, out_sems):
    loads = [
        pltpu.make_async_copy(ref.at[1], ins.at[n], in_sems.at[n]) for n, ref in enumerate((keep_a, got_a, keep_b, got_b))
    ]
    start_all(loads)
    wait_all(loads)
    for n in range(2):
        sums[n] = (ins[2 * n].astype(F32) + ins[2 * n + 1].astype(F32)).astype(BF)
    stores = [pltpu.make_async_copy(sums.at[n], ref.at[0], out_sems.at[n]) for n, ref in enumerate((out_b, out_a))]
    start_all(stores)
    wait_all(stores)


def finish_rows_kernel(spread, keep, got, out_t):
    width = out_t.shape[0]
    total = (keep[...].astype(F32) + got[...].astype(F32)).T
    if spread:
        block = width // 8
        total = jnp.concatenate([total[i * PAD : i * PAD + block] for i in range(8)], axis=0)
    out_t[...] = total[:width].astype(BF)


def finish_gate_up_kernel(spot, gate_keep, gate_far, up_keep, up_far, out):
    core = spot[0]
    block = out.shape[0]
    parts = []
    for keep, far in ((gate_keep, gate_far), (up_keep, up_far)):
        mine = keep[...].astype(F32)[:block]
        theirs = far[...].astype(F32)[:block]
        even = jnp.where(core == 0, mine, theirs)
        odd = jnp.where(core == 0, theirs, mine)
        for j in range(4):
            for p in (even, odd):
                at = j * PAD
                parts += [p[:, at : at + MAIN], p[:, at + 164 : at + 176], p[:, at + 180 : at + PAD]]
    out[...] = jnp.concatenate(parts, axis=1).reshape(out.shape)


def finish_down_kernel(keep_a, got_a, last_a, keep_b, got_b, last_b, out):
    def total(keep, got, last):
        return keep[0].astype(F32) + got[0].astype(F32) + last[...].astype(F32)

    rows = jnp.concatenate([total(keep_a, got_a, last_a), total(keep_b, got_b, last_b)], axis=0)
    rows = jnp.concatenate([rows[:MAIN], rows[164:176], rows[180:]], axis=0)
    out[...] = rows[:, : out.shape[2]].reshape(out.shape)


VMEM = pl.BlockSpec(memory_space=pltpu.VMEM)
SMEM = pl.BlockSpec(memory_space=pltpu.SMEM)
ANY = pl.BlockSpec(memory_space=pl.ANY)


def call(body, in_specs, out_specs, out_shape, scratch=(), mib=50, flops=1000, aliases=None):
    return pl.pallas_call(
        body,
        in_specs=in_specs,
        out_specs=out_specs,
        out_shape=out_shape,
        scratch_shapes=list(scratch),
        input_output_aliases=aliases or {},
        compiler_params=pltpu.CompilerParams(vmem_limit_bytes=mib * MIB),
        cost_estimate=pl.CostEstimate(flops=flops, bytes_accessed=1000, transcendentals=0),
    )


def paired(tokens, expert_ids, combine_weights, out_grad, w_gate_up, w_down):
    count, top = expert_ids.shape
    width = tokens.shape[1]
    scale = 1.0 / math.sqrt(8 * count * top)
    place = lax.axis_index("dp")
    line = lax.axis_index("expert")
    core = place % 2
    spot = jnp.stack([core, place // 2, line]).astype(jnp.int32)
    block = w_gate_up.shape[1]
    full = 8 * PAD
    units = 4 * PAD
    rows = 8 * count
    dma = pltpu.SemaphoreType.DMA

    def swap(bit):
        pairs = [(i, i ^ bit) for i in range(8)]
        return lambda value: lax.ppermute(value, "dp", pairs)

    over_core, over_x, over_y = swap(1), swap(2), swap(4)

    def onward(value):
        return lax.ppermute(value, "expert", [(i, (i + 1) % 4) for i in range(4)])

    def backward(value):
        return lax.ppermute(value, "expert", [(i, (i + 3) % 4) for i in range(4)])

    def array(*shape):
        return jax.ShapeDtypeStruct(shape, BF)

    def held(*shape):
        return pltpu.VMEM(shape, BF)

    def together(*values):
        return lax.optimization_barrier(values)

    xg0 = call(prepare_rows_kernel, [VMEM] * 4, VMEM, array(count, 2 * full), mib=60)(
        tokens.T, out_grad.T, expert_ids.T, combine_weights.T
    )
    own, other, high = call(
        prepare_weights_kernel,
        [SMEM] + [VMEM] * 2,
        [VMEM] * 3,
        [array(PAD + LOT, full), array(PAD, full), array(LOT, full)],
        mib=60,
    )(spot, w_gate_up[0], w_down[0])

    other, own_x, own_y, xg1, fxg0 = over_core(other), over_x(own), over_y(own), onward(xg0), over_core(xg0)
    other = call(join_kernel, [VMEM] * 3, VMEM, array(PAD + LOT, full))(other, high, w_down[0])
    own_x, own_y, other, fxg0 = together(own_x, own_y, other, fxg0)
    other_x, other_y, xg2, fxg1 = over_x(other), over_y(other), onward(xg1), over_core(xg1)
    other_x, other_y, own_x = together(other_x, other_y, own_x)
    own_xy, other_xy, xg3, fxg2 = over_y(own_x), over_x(other_y), onward(xg2), over_core(xg2)
    fxg3 = over_core(xg3)

    owns = (own, own_x, own_y, own_xy)
    others = (other, other_x, other_y, other_xy)
    xs = (xg0, xg1, xg2, xg3, fxg0, fxg1, fxg2, fxg3)
    row_shapes = [array(rows // 2, full), array(count, full), array(3 * count, full)]
    up_f, gate_f, grad, out_own, out_first, out_rest, *down_parts = call(
        functools.partial(forward_kernel, scale),
        [SMEM] + [ANY] * 16,
        [ANY] * 10,
        [array(rows, units)] * 2 + [array(rows, full)] + row_shapes + [array(2, HALF, full)] * 4,
        [held(full, full), held(units, full), held(rows, full), held(rows, full)]
        + [held(rows, units)] * 3
        + [pltpu.VMEM((rows, 128), F32), held(rows, full), held(units, full)]
        + [dma((8,)), dma((16,)), dma((8,)), dma((8,)), dma((12,)), dma((3,)), dma((8,))],
        flops=LONG,
    )(spot, *owns, *others, *xs)

    def slot_sum(own_part, far_part, s, far):
        return own_part[s * count : (s + 1) * count].astype(F32) + far_part[far * count : (far + 1) * count].astype(F32)

    def after(value, moving):
        return (value + moving.astype(F32)).astype(BF)

    def first_step(parts):
        return over_x(parts[0]), over_y(parts[2])

    def passed_on(parts, got):
        def add(a, b):
            return (a[1].astype(F32) + b[1].astype(F32)).astype(BF)

        return add(parts[1], got[0]), add(parts[3], got[1])

    def second_step(away):
        return over_y(away[0]), over_x(away[1])

    def totals(parts, got, last):
        def add(a, b, c):
            return a[0].astype(F32) + b[0].astype(F32) + c.astype(F32)

        return add(parts[1], got[0], last[0]), add(parts[3], got[1], last[1])

    down_got = first_step(down_parts)
    m1 = slot_sum(out_own, over_core(out_first), 3, 0).astype(BF)
    m1, grad = together(m1, grad)
    m1 = backward(m1)
    out_rest = over_core(out_rest)
    pre_grad, *gate_parts = call(
        functools.partial(gate_grad_kernel, scale),
        [SMEM] + [ANY] * 19,
        [ANY] * 5,
        [array(rows, full)] + [array(2, PAD, units)] * 4,
        [held(units, full), held(rows, full), held(rows, units), held(rows, units), held(rows, full)]
        + [held(rows, full), held(full, units), dma((16,)), dma((12,)), dma((8,)), dma((4,)), dma((8,))],
        flops=LONG,
    )(spot, *owns, *others, grad, up_f, gate_f, *xs)
    *down_got, m1, pre_grad, gate_a, gate_b, out_rest = together(
        *down_got, m1, pre_grad, gate_parts[0], gate_parts[2], out_rest
    )
    m2 = backward(after(slot_sum(out_own, out_rest, 2, 2), m1))
    down_last = second_step(passed_on(down_parts, down_got))
    gate_got = over_x(gate_a), over_y(gate_b)
    in_own, in_first, in_rest, *up_parts = call(
        functools.partial(up_grad_kernel, scale),
        [SMEM] + [ANY] * 17,
        [ANY] * 7,
        row_shapes + [array(3, PAD, units), array(2, PAD, units)] * 2,
        [held(full, full), held(rows, full), held(rows, full), held(full, units), held(rows, full)]
        + [dma((8,)), dma((8,)), dma((4,)), dma((4,)), dma((8,))],
        flops=LONG,
    )(spot, *owns, *others, *xs, pre_grad)
    m2, in_first, in_rest, l1, l2, g1, g2, up_a, up_b = together(
        m2, in_first, in_rest, *down_last, *gate_got, up_parts[0], up_parts[2]
    )
    down_last, gate_got = (l1, l2), (g1, g2)
    m3 = after(slot_sum(out_own, out_rest, 1, 1), m2)
    up_a, up_b = call(
        pass_kernel,
        [ANY] * 6,
        [ANY] * 2,
        [array(3, PAD, units)] * 2,
        [held(4, PAD, units), held(2, PAD, units), dma((4,)), dma((2,))],
        aliases={4: 0, 5: 1},
    )(gate_parts[1], gate_got[0], gate_parts[3], gate_got[1], up_a, up_b)
    up_a, up_b, m3, in_first, in_rest = together(up_a, up_b, m3, in_first, in_rest)
    by_y, by_x, m3 = over_y(up_b), over_x(up_a), backward(m3)
    i1 = backward(slot_sum(in_own, over_core(in_first), 3, 0).astype(BF))
    in_rest = over_core(in_rest)

    def finish_rows(value, moving, spread):
        return call(functools.partial(finish_rows_kernel, spread), [VMEM] * 2, VMEM, array(width, count))(value, moving).T

    grad_down = call(
        finish_down_kernel, [VMEM] * 6, VMEM, jax.ShapeDtypeStruct((block, 1, width), F32)
    )(down_parts[1], down_got[0], down_last[0], down_parts[3], down_got[1], down_last[1])
    by_x, by_y, m3, grad_down = together(by_x, by_y, m3, grad_down)
    up_got, gate_last = (by_x[1:], by_y[1:]), (by_y[0], by_x[0])
    i2 = backward(after(slot_sum(in_own, in_rest, 2, 2), i1))
    up_last = second_step(passed_on(up_parts, up_got))

    def split(parts, got, last):
        a, b = totals(parts, got, last)
        return jnp.where(core == 0, a, b), over_core(jnp.where(core == 0, b, a).astype(BF))

    gate_keep, gate_far = split(gate_parts, gate_got, gate_last)
    i3 = after(slot_sum(in_own, in_rest, 1, 1), i2)
    mixed_out = finish_rows(slot_sum(out_own, out_rest, 0, 0), m3, False)
    l1, l2, gate_keep, gate_far, mixed_out, _ = together(*up_last, gate_keep, gate_far, mixed_out, i3)
    i3 = backward(i3)
    up_keep, up_far = split(up_parts, up_got, (l1, l2))
    grad_gate_up = call(
        finish_gate_up_kernel,
        [SMEM] + [VMEM] * 4,
        VMEM,
        jax.ShapeDtypeStruct((block, 1, 2 * width), F32),
    )(spot, gate_keep, gate_far, up_keep, up_far)
    token_grad = finish_rows(slot_sum(in_own, in_rest, 0, 0), i3, True)
    return (mixed_out, token_grad, grad_gate_up.transpose(1, 0, 2), grad_down.transpose(1, 0, 2))


def solution(mesh):
    placed = (
        P(("dp", "expert"), None),
        P(("dp", "expert"), None),
        P(("dp", "expert"), None),
        P(("dp", "expert"), None),
        P("expert", "dp", None),
        P("expert", "dp", None),
    )
    small = mesh.shape["dp"] == 8 and mesh.shape["expert"] == 4
    return jax.shard_map(
        paired if small else general,
        mesh=mesh,
        in_specs=placed,
        out_specs=(
            P(("dp", "expert"), None),
            P(("dp", "expert"), None),
            P("expert", "dp", None),
            P("expert", "dp", None),
        ),
        check_vma=False,
    )
```
